128 devices in a mesh: band: 4 (over z), tile: 32 (over x, y, core).
Axes of the slice: x: 4, y: 4, z: 4, core: 2. Of those that a mesh axis runs over, the one named last changes fastest.
Arguments:
- increment: float32 [64, 5, 256, 768], P('band', None, 'tile'), may hold values from -6 to 6
- courant_x: float32 [64, 256, 768], P('band', 'tile'), may hold values from -0.45 to 0.45
- courant_y: float32 [64, 256, 768], P('band', 'tile'), may hold values from -0.45 to 0.45
- level_inverse: float32 [5, 64, 16], P(None, 'band'), may hold values from -0.25 to 1.25, as said below
- coupling: float32 [5], replicated, may hold values from 0.5 to 2
- profile: float32 [64, 5, 64], P('band'), may hold values from -0.3125 to 0.3125
- send_column: int32 [32, 8192], P('tile'), may hold values from 0 to 6143
- send_block: int32 [32, 8192], P('tile'), may hold values from 0 to 63
- send_count: int32 [32, 32], P('tile'), may hold values from 1 to 256, as said below
- obs_weight: float32 [32, 8192], P('tile'), may hold values from 1 to 10
Outputs:
- hessian: float32 [64, 5, 256, 768], P('band', None, 'tile')
The draws below stay inside these ranges and needn't reach their ends.
Inputs may be any that keep to these rules, and one draw needn't show every extreme that they name: `level_inverse`: rows b * 16 to b * 16 + 15 of each variable hold the block of band b. `send_column`: column index within the sending tile's own rows. Row t, column d: the slots k < send_count[t, d] of the group sent from tile t to owner d are live; in every draw some owner receives 256 from every tile.
All inputs are finite; a program needn't handle non-finite values.
Results may differ from the reference program's by a relative error of at most 0.0001.
Values sent between devices are 32-bit elements; how exact they have to be, the bound alone decides.
A program may use at most 64 MiB of HBM per device.

```python
import math
import jax
import jax.numpy as jnp
from jax import lax

VARS = 5
LEVB = 16
NX = 768
ROWS_DEV = 8
CAP = 256
NBLK = 64
LEV = 64
NY = 256
TILES = 32
N_BAND = 4
N_TILE = 32


def draw_level_inverse(key, part):
    key = jax.random.fold_in(key, 5)
    first_key, second_key = jax.random.split(key)
    diagonal = jax.random.uniform(first_key, (VARS, LEV, 1), jnp.float32, 0.6, 1.0)
    offdiag = jax.random.uniform(second_key, (VARS, LEV, LEVB), jnp.float32, -0.25, 0.25)
    position = jnp.arange(LEV) % LEVB
    identity = (position[:, None] == jnp.arange(LEVB)[None, :]).astype(jnp.float32)
    return identity[None] * diagonal + offdiag


def draw_send_count(key, part):
    key = jax.random.fold_in(key, 11)
    first_key, second_key, third_key = jax.random.split(key, 3)
    heavier = jax.random.randint(first_key, (TILES,), 0, 4)
    popular = jnp.where(heavier == 0, 4, 1)
    baseline = jax.random.randint(second_key, (TILES, TILES), CAP // 6, CAP // 3 + 1)
    counts = jnp.minimum(baseline * popular[None, :], CAP)
    hottest = jax.random.randint(third_key, (), 0, TILES)
    counts = jnp.where(jnp.arange(TILES)[None, :] == hottest, CAP, counts)
    return counts.astype(jnp.int32)


def plant(entries, own_key, low, largest):
    extent = entries.shape
    spot = [jax.random.randint(jax.random.fold_in(own_key, axis), (), 0, extent[axis]) for axis in range(len(extent))]
    entries = entries.at[tuple(spot)].set(low)
    longest = extent.index(max(extent))
    spot[longest] = (spot[longest] + 1) % extent[longest]
    return entries.at[tuple(spot)].set(largest)


def levels(key, dims, cuts, low, top_value):
    def one(dim, parts):
        draws = jax.random.uniform(jax.random.fold_in(jax.random.fold_in(key, 6), dim), (parts,), jnp.float32, low / len(cuts), top_value / len(cuts))
        return jnp.repeat(jnp.exp(draws), dims[dim] // parts).reshape((-1,) + (1,) * (len(dims) - dim - 1))

    factor_of = one(*cuts[0])
    for cut in cuts[1:]:
        factor_of = factor_of * one(*cut)
    return factor_of


def scatter_about(own_key, extent, width, most, pieces=(), kind=jnp.bfloat16):
    array = jax.random.normal(own_key, extent, jnp.float32) * width
    if len(pieces) > 0:
        array = levels(own_key, extent, pieces, -0.22, 0.18) * array
    return jnp.clip(array, min=-most, max=most).astype(kind)


def setup_inputs(seed: int = 0) -> dict:
    seeds = jax.random.split(jax.random.key(seed), 11)
    return {
        "increment": scatter_about(seeds[0], (LEV, VARS, NY, NX), 1.0, 6.0, ((0, 4), (2, 32)), jnp.float32),
        "courant_x": jnp.clip(jax.random.uniform(seeds[1], (LEV, NY, NX), jnp.float32, -0.45, 0.45) * levels(seeds[1], (LEV, NY, NX), ((0, 4), (1, 32)), -0.4, 0.0), -0.45, 0.45),
        "courant_y": jnp.clip(jax.random.uniform(seeds[2], (LEV, NY, NX), jnp.float32, -0.45, 0.45) * levels(seeds[2], (LEV, NY, NX), ((0, 4), (1, 32)), -0.4, 0.0), -0.45, 0.45),
        "level_inverse": draw_level_inverse(jax.random.fold_in(seeds[10], 71), 0),
        "coupling": jnp.clip(jnp.exp(jax.random.uniform(seeds[4], (VARS,), jnp.float32, math.log(0.5), math.log(2.0))), 0.5, 2.0),
        "profile": scatter_about(seeds[5], (LEV, VARS, NBLK), (LEV * VARS) ** -0.5, 0.3125, ((0, 4),), jnp.float32),
        "send_column": plant(jax.random.randint(seeds[6], (TILES, TILES * CAP), 0, ROWS_DEV * NX), jax.random.fold_in(seeds[6], 1), 0, (ROWS_DEV * NX) - 1).astype(jnp.int32),
        "send_block": plant(jax.random.randint(seeds[7], (TILES, TILES * CAP), 0, NBLK), jax.random.fold_in(seeds[7], 1), 0, NBLK - 1).astype(jnp.int32),
        "send_count": draw_send_count(jax.random.fold_in(seeds[10], 71), 0),
        "obs_weight": jnp.clip(jnp.exp(math.log(10.0) - 2.3025851 * jax.random.uniform(seeds[9], (TILES, TILES * CAP), jnp.float32) ** levels(seeds[9], (TILES, TILES * CAP), ((0, 32),), -0.2, 0.2)), 1.0, 10.0),
    }


exact_precision = lax.Precision.HIGHEST

def upwind(courant):
    return ((jnp.abs(courant) + courant) * 0.5, (jnp.abs(courant) - courant) * 0.5)

def advect(current, courant_x, courant_y):
    from_west, from_east = upwind(courant_x[:, None])
    from_south, from_north = upwind(courant_y[:, None])
    padded = jnp.pad(current, ((0, 0), (0, 0), (1, 1), (1, 1)))
    centre = padded[:, :, 1:-1, 1:-1]
    keep = 1.0 - from_west - from_east - from_south - from_north
    return keep * centre + from_west * padded[:, :, 1:-1, :-2] + from_east * padded[:, :, 1:-1, 2:] + from_south * padded[:, :, :-2, 1:-1] + from_north * padded[:, :, 2:, 1:-1]

def vertical(current, level_inverse, coupling):
    bands = current.reshape(N_BAND, LEVB, VARS, NY, NX)
    inverse = level_inverse.reshape(VARS, N_BAND, LEVB, LEVB)
    carried = jnp.zeros((VARS, NY, NX), jnp.float32)
    solved_list = []
    for band_index in range(N_BAND):
        block = inverse[:, band_index]
        solved = jnp.einsum('vij,jvyx->ivyx', block, bands[band_index], precision=exact_precision)
        solved = solved + jnp.einsum('vi,vyx->ivyx', coupling[:, None] * block[:, :, 0], carried, precision=exact_precision)
        carried = solved[LEVB - 1]
        solved_list.append(solved)
    carried = jnp.zeros((VARS, NY, NX), jnp.float32)
    results = [None] * N_BAND
    for band_index in range(N_BAND - 1, -1, -1):
        block = inverse[:, band_index]
        result = solved_list[band_index] + jnp.einsum('vi,vyx->ivyx', coupling[:, None] * block[:, :, LEVB - 1], carried, precision=exact_precision)
        carried = result[0]
        results[band_index] = result
    return jnp.concatenate(results, axis=0)

def observe(state, profile, send_column, send_block):
    level_vars = LEV * VARS
    tiled = state.reshape(LEV, VARS, N_TILE, ROWS_DEV * NX).transpose(2, 0, 1, 3).reshape(N_TILE, level_vars, ROWS_DEV * NX)
    profile_table = profile.reshape(level_vars, NBLK)

    def per_tile(element):
        tile_field, columns, blocks = element
        return lax.optimization_barrier(jnp.sum(jnp.take(tile_field, columns, axis=1) * jnp.take(profile_table, blocks, axis=1), 0))
    return lax.map(per_tile, (tiled, send_column, send_block))

def observe_adjoint(weighted, profile, send_column, send_block):
    level_vars = LEV * VARS
    profile_table = profile.reshape(level_vars, NBLK)

    def per_tile(element):
        weights, columns, blocks = element
        chosen = jnp.take(profile_table, blocks, axis=1) * weights[None, :]
        return jnp.zeros((level_vars, ROWS_DEV * NX), jnp.float32).at[:, columns].add(chosen)
    tiled = lax.map(per_tile, (weighted, send_column, send_block))
    return tiled.reshape(N_TILE, LEV, VARS, ROWS_DEV * NX).transpose(1, 2, 0, 3).reshape(LEV, VARS, NY, NX)

def reference(increment, courant_x, courant_y, level_inverse, coupling, profile, send_column, send_block, send_count, obs_weight):

    def model(current):
        for repeat_index in range(2):
            current = vertical(advect(current, courant_x, courant_y), level_inverse, coupling)
        return current
    state, pullback = jax.vjp(model, increment)
    model_values = observe(state, profile, send_column, send_block)
    slot_index = jnp.arange(CAP).astype(jnp.int32)
    live_mask = (slot_index[None, None, :] < send_count[:, :, None]).astype(jnp.float32).reshape(N_TILE, N_TILE * CAP)
    home_weight = obs_weight.reshape(N_TILE, N_TILE, CAP).transpose(1, 0, 2).reshape(N_TILE, N_TILE * CAP)
    weighted = live_mask * home_weight * model_values
    state_adjoint = observe_adjoint(weighted, profile, send_column, send_block)
    adjoint = pullback(state_adjoint)[0]
    return increment + adjoint
```

```python
import functools

import jax
import jax.numpy as jnp
from jax import lax
from jax.experimental import pallas as pl
from jax.experimental.pallas import tpu as pltpu
from jax.sharding import PartitionSpec as P

MESH = pl.DeviceIdType.MESH
VARS = 5
LEVB = 16
LV = VARS * LEVB
ROWS = 8
NX = 768
BANDS = 4
TILES = 32
CHUNK = 256
CHUNKS = 32
WIDE = 256
WINDOWS = 24
PAIRS = 56
NBLK = 64
ORDER = (1, 2, 3, 4, 5, 6, 0, 7)
SPLIT = 24
F32 = jnp.float32
BF16 = jnp.bfloat16


def halves(value):
    high = value.astype(BF16)
    low = (value - high.astype(F32)).astype(BF16)
    return high, low


def mm(a, b):
    return jnp.dot(a, b, preferred_element_type=F32)


def kernel(
    inc_ref, cx_ref, cy_ref, mats_ref, cols_ref, coef_ref, prof_ref, cell_ref, blk_ref, wgt_ref, pair_ref,
    out_ref,
    field, cyh, co, adj, local, stack, mext, edges, recv, coefs, ps, xs, onehot, val, valr, acc,
    halo_s, halo_r, cy_s, cy_r, cf_s, cf_r, ed_s, ed_r, va_s, va_r,
):
    band = lax.axis_index("band")
    tile = lax.axis_index("tile")
    north = lax.rem(tile + 1, TILES)
    south = lax.rem(tile + TILES - 1, TILES)
    partner = [lax.rem(band + o, BANDS) for o in (1, 2, 3)]

    barrier = pltpu.get_barrier_semaphore()
    for t in (north, south):
        pl.semaphore_signal(barrier, inc=1, device_id={"tile": t}, device_id_type=MESH)
    for p in partner:
        pl.semaphore_signal(barrier, inc=1, device_id={"band": p}, device_id_type=MESH)
    pl.semaphore_wait(barrier, 5)

    sent = []

    def halo(buffer, send, receive):
        up = pltpu.make_async_remote_copy(
            buffer.at[ROWS], buffer.at[0], send.at[0], receive.at[0],
            device_id={"tile": north}, device_id_type=MESH)
        down = pltpu.make_async_remote_copy(
            buffer.at[1], buffer.at[ROWS + 1], send.at[1], receive.at[1],
            device_id={"tile": south}, device_id_type=MESH)
        up.start()
        down.start()
        sent.extend([up, down])
        return up, down

    def band_copy(source, target, send, receive, o):
        copy = pltpu.make_async_remote_copy(
            source, target, send, receive, device_id={"band": partner[o]}, device_id_type=MESH)
        copy.start()
        sent.append(copy)
        return copy

    for v in range(VARS):
        turned = jnp.swapaxes(inc_ref[:, v], 0, 1)
        field[0, 1:ROWS + 1, LEVB * v:LEVB * v + LEVB, :] = turned
    halo1 = halo(field.at[0], halo_s.at[0], halo_r.at[0])
    coefs[0] = coef_ref[...]
    cf_copies = [
        band_copy(coefs.at[0], coefs.at[o + 1], cf_s.at[o], cf_r.at[o], o) for o in range(3)
    ]
    cyh[1:ROWS + 1] = jnp.swapaxes(cy_ref[...], 0, 1)
    halo_cy = halo(cyh, cy_s, cy_r)
    co[0] = jnp.swapaxes(cx_ref[...], 0, 1)

    lane = lax.broadcasted_iota(jnp.int32, (LEVB, NX), 1)
    for y in range(ROWS):
        cx = co[0, y]
        cy = cyh[y + 1]
        ax, bx = (jnp.abs(cx) + cx) * 0.5, (jnp.abs(cx) - cx) * 0.5
        ay, by = (jnp.abs(cy) + cy) * 0.5, (jnp.abs(cy) - cy) * 0.5
        co[0, y] = 1.0 - ax - bx - ay - by
        co[1, y] = jnp.where(lane == 0, 0.0, ax)
        co[2, y] = jnp.where(lane == NX - 1, 0.0, bx)
        if y == 0:
            ay = jnp.where(tile == 0, 0.0, ay)
        if y == ROWS - 1:
            by = jnp.where(tile == TILES - 1, 0.0, by)
        co[3, y] = ay
        co[4, y] = by
        adj[0, y] = jnp.where(lane == 0, 0.0, pltpu.roll(bx, 1, 1))
        adj[1, y] = jnp.where(lane == NX - 1, 0.0, pltpu.roll(ax, NX - 1, 1))

    profiles = jnp.concatenate(halves(prof_ref[...]), axis=0)
    block_iota = lax.broadcasted_iota(jnp.int32, (NBLK, CHUNK), 0)

    def pick_profiles(c, carry):
        hot = (block_iota == blk_ref[c]).astype(BF16)
        picked = mm(profiles, hot)
        ps[c] = picked[:LV] + picked[LV:]
        return carry

    lax.fori_loop(0, CHUNKS, pick_profiles, 0)

    for copy in cf_copies:
        copy.wait_recv()

    def of_band(lane_index):
        result = []
        for j in range(BANDS):
            total = jnp.zeros((8, 1), F32)
            for b in range(BANDS):
                entry = coefs[(b - j) % BANDS][:, lane_index:lane_index + 1]
                total = total + jnp.where(band == b, entry, 0.0)
            result.append(total)
        return result

    def select(values):
        total = jnp.zeros((8, 1), F32)
        for b in range(BANDS):
            total = total + jnp.where(band == b, values[b], 0.0)
        return total

    k0, k15, g0 = of_band(0), of_band(1), of_band(2)
    zero = jnp.zeros((8, 1), F32)

    def chain(a, g):
        e = [zero] * (BANDS + 1)
        for j in range(BANDS - 1, -1, -1):
            e[j] = k0[j] + g[j] * e[j + 1] * a[j]
        into_first = select([g[b] * e[b + 1] for b in range(BANDS)])
        own = select([e[b + 1] for b in range(BANDS)])
        low, high = [], []
        for o in (1, 2, 3):
            t_list, s_list = [], []
            for b in range(BANDS):
                j = (b - o) % BANDS
                factor = zero + 1.0
                if j < b:
                    for k in range(j + 1, b):
                        factor = factor * a[k]
                    t_list.append(factor)
                    s_list.append(e[b + 1] * a[b] * factor)
                else:
                    for k in range(b + 1, j):
                        factor = factor * g[k]
                    t_list.append(zero)
                    s_list.append(factor)
            low.append(select(t_list))
            high.append(select(s_list))
        return into_first, own, low, high

    chains = (chain(k15, g0), chain(g0, k15))
    for kind in range(2):
        matrix = mats_ref[kind]
        last = matrix[LV:LV + 8]
        first = matrix[LV + 8:LV + 16] + chains[kind][0] * last
        matrix = jnp.concatenate([matrix[:LV + 8], first], axis=0)
        high, low = halves(matrix)
        mext[kind, 0] = high
        mext[kind, 1] = low

    def stencil(src, y, v, kind):
        rows = slice(LEVB * v, LEVB * v + LEVB)
        f = field[src, y + 1, rows, :]
        west, east = pltpu.roll(f, 1, 1), pltpu.roll(f, NX - 1, 1)
        if kind == 0:
            cw, ce, cs, cn = (co[i, y] for i in (1, 2, 3, 4))
        else:
            cw, ce, cs, cn = adj[0, y], adj[1, y], adj[2, y], adj[3, y]
        return (
            co[0, y] * f + cw * west + ce * east
            + cs * field[src, y, rows, :] + cn * field[src, y + 2, rows, :]
        )

    def solve(stage, kind, row_value, before_last, store_row, after_edges):
        copies = []
        for k, y in enumerate(ORDER):
            if k == 6:
                before_last()
            for v in range(VARS):
                high, low = halves(row_value(y, v))
                rows = slice(LEVB * v, LEVB * v + LEVB)
                stack[k % 2, 0, rows, :] = high
                stack[k % 2, 1, rows, :] = low
            high, low = stack[k % 2, 0], stack[k % 2, 1]
            lhs = jnp.concatenate([mext[kind, 0], mext[kind, 1]], axis=0)
            first = mm(lhs, high)
            result = first[:LV + 16] + first[LV + 16:] + mm(mext[kind, 0], low)
            local[y] = result[:LV]
            edges[stage, 0, VARS * k:VARS * k + VARS, :] = result[LV:LV + VARS]
            edges[stage, 1, VARS * k:VARS * k + VARS, :] = result[LV + 8:LV + 8 + VARS]
            for part, (at, lo, hi) in enumerate(((4, 0, SPLIT), (7, SPLIT, VARS * ROWS))):
                if k == at:
                    for o in range(3):
                        above = (band + o + 1) // BANDS
                        copies.append(band_copy(
                            edges.at[stage, above, lo:hi], recv.at[stage, o, lo:hi],
                            ed_s.at[stage, o, part], ed_r.at[stage, o, part], o))
        for copy in copies:
            copy.wait_recv()
        _, own, low_c, high_c = chains[kind]
        left, right = cols_ref[kind, :, 0:1], cols_ref[kind, :, 1:2]
        for y in (0, 7, 1, 2, 3, 4, 5, 6):
            k = ORDER.index(y)
            span = slice(VARS * k, VARS * k + VARS)
            t = jnp.zeros((VARS, NX), F32)
            s = own[:VARS] * edges[stage, 0, span, :]
            for o in range(3):
                got = recv[stage, o, span, :]
                t = t + low_c[o][:VARS] * got
                s = s + high_c[o][:VARS] * got
            for v in range(VARS):
                rows = slice(LEVB * v, LEVB * v + LEVB)
                store_row(y, v, local[y, rows, :] + left[rows] * t[v:v + 1] + right[rows] * s[v:v + 1])
            if y == 7:
                after_edges()

    pending = {}

    def wait_halo(copies):
        for copy in copies:
            copy.wait_recv()

    def into_field(index):
        def store(y, v, value):
            field[index, y + 1, LEVB * v:LEVB * v + LEVB, :] = value
        return store

    def send_field(index):
        def send():
            pending[index] = halo(field.at[index], halo_s.at[index], halo_r.at[index])
        return send

    def store_state(y, v, value):
        high, low = halves(value)
        for j in range(3):
            cols = slice(WIDE * j, WIDE * j + WIDE)
            xs[3 * y + j, LEVB * v:LEVB * v + LEVB, :] = high[:, cols]
            xs[3 * y + j, LV + LEVB * v:LV + LEVB * v + LEVB, :] = low[:, cols]

    solve(0, 0, lambda y, v: stencil(0, y, v, 0), lambda: wait_halo(halo1), into_field(1), send_field(1))
    solve(1, 0, lambda y, v: stencil(1, y, v, 0), lambda: wait_halo(pending[1]), store_state, lambda: None)

    cell_iota = lax.broadcasted_iota(jnp.int32, (WIDE, CHUNK), 0)

    def observe(p, carry):
        c, w, base = pair_ref[0, p], pair_ref[1, p], pair_ref[2, p]
        hot = (cell_iota == cell_ref[c] - base).astype(BF16)
        onehot[p] = hot
        picked = mm(xs[w], hot)
        product = (picked[:LV] + picked[LV:]) * ps[c]
        val[p] = jnp.sum(product, axis=0, keepdims=True)
        return carry

    lax.fori_loop(0, PAIRS, observe, 0)
    copies = [band_copy(val, valr.at[o], va_s.at[o], va_r.at[o], o) for o in range(3)]

    wait_halo(halo_cy)
    for y in range(ROWS):
        below, above = cyh[y], cyh[y + 2]
        by = (jnp.abs(below) - below) * 0.5
        ay = (jnp.abs(above) + above) * 0.5
        if y == 0:
            by = jnp.where(tile == 0, 0.0, by)
        if y == ROWS - 1:
            ay = jnp.where(tile == TILES - 1, 0.0, ay)
        adj[2, y] = by
        adj[3, y] = ay
    for copy in copies:
        copy.wait_recv()

    def spread(p, before):
        c, same = pair_ref[0, p], pair_ref[3, p]
        values = (val[p] + valr[0, p]) + (valr[1, p] + valr[2, p])
        high, low = halves(ps[c] * (values * wgt_ref[c]))
        both = jnp.concatenate([high, low], axis=0)
        added = lax.dot_general(both, onehot[p], (((1,), (1,)), ((), ())), preferred_element_type=F32)
        total = before * same.astype(F32) + (added[:LV] + added[LV:])
        acc[p] = total
        return total

    lax.fori_loop(0, PAIRS, spread, jnp.zeros((LV, WIDE), F32))

    def gradient(y, v):
        parts = []
        for j in range(3):
            w = 3 * y + j
            some = pair_ref[5, w].astype(F32)
            parts.append(acc[pair_ref[4, w], LEVB * v:LEVB * v + LEVB, :] * some)
        return jnp.concatenate(parts, axis=1)

    solve(2, 1, gradient, lambda: None, into_field(2), send_field(2))
    solve(3, 1, lambda y, v: stencil(2, y, v, 1), lambda: wait_halo(pending[2]), into_field(3), send_field(3))

    for k, y in enumerate(ORDER):
        if k == 6:
            wait_halo(pending[3])
        for v in range(VARS):
            result = stencil(3, y, v, 1) + field[0, y + 1, LEVB * v:LEVB * v + LEVB, :]
            local[y, LEVB * v:LEVB * v + LEVB, :] = result
    for v in range(VARS):
        out_ref[:, v] = jnp.swapaxes(local[:, LEVB * v:LEVB * v + LEVB, :], 0, 1)
    for copy in sent:
        copy.wait_send()


def block_diagonal(blocks):
    eye = jnp.eye(VARS, dtype=F32)
    return (eye[:, None, :, None] * blocks[:, :, None, :]).reshape(VARS * blocks.shape[1], -1)


def shards(
    increment, courant_x, courant_y, level_inverse, coupling, profile, send_column, send_block, send_count, obs_weight,
):
    inverse = level_inverse
    scale = coupling[:, None]
    pad3 = jnp.zeros((3, LV), F32)

    def extended(main, last, first):
        return jnp.concatenate(
            [block_diagonal(main), block_diagonal(last[:, None]), pad3, block_diagonal(first[:, None]), pad3])

    first_column, last_column = scale * inverse[:, :, 0], scale * inverse[:, :, LEVB - 1]
    mats = jnp.stack([
        extended(inverse, inverse[:, LEVB - 1], inverse[:, 0]),
        extended(inverse.transpose(0, 2, 1), last_column, first_column),
    ])
    cols = jnp.stack([
        jnp.stack([first_column.reshape(LV), last_column.reshape(LV)], axis=1),
        jnp.stack([inverse[:, 0].reshape(LV), inverse[:, LEVB - 1].reshape(LV)], axis=1),
    ])
    cols = jnp.pad(cols, ((0, 0), (0, 0), (0, 126)))
    coef = jnp.stack([first_column[:, 0], first_column[:, LEVB - 1], last_column[:, 0]], axis=1)
    coef = jnp.pad(coef, ((0, 3), (0, 125)))
    table = profile.transpose(1, 0, 2).reshape(LV, NBLK)

    weight = lax.all_to_all(obs_weight.reshape(TILES, -1), "tile", split_axis=0, concat_axis=0, tiled=True)
    slot = lax.broadcasted_iota(jnp.int32, weight.shape, 1)
    weight = jnp.where(slot < send_count.reshape(TILES)[:, None], weight, 0.0)
    key = send_column[0] * NBLK + send_block[0]
    key, weight = lax.sort((key, weight.reshape(-1)), num_keys=1)
    cell, blk = (key // NBLK).reshape(CHUNKS, CHUNK), (key % NBLK).reshape(CHUNKS, CHUNK)
    weight = weight.reshape(CHUNKS, CHUNK)
    first, last = cell[:, 0] // WIDE, cell[:, CHUNK - 1] // WIDE
    number = last - first + 1
    order = jnp.arange(CHUNKS)
    start = jnp.sum(jnp.where(order[None, :] < order[:, None], number[None, :], 0), axis=1)
    p = jnp.arange(64)
    chunk = jnp.sum((start[None, :] <= p[:, None]).astype(jnp.int32), axis=1) - 1
    mine = chunk[:, None] == order[None, :]
    window = jnp.sum(jnp.where(mine, first[None, :] - start[None, :], 0), axis=1) + p
    valid = p < jnp.sum(number)
    window_index = jnp.where(valid, window, WINDOWS - 1)
    base = jnp.where(valid, window * WIDE, -(1 << 20))
    same = jnp.concatenate([jnp.zeros((1,), jnp.int32), (window_index[1:] == window_index[:-1]).astype(jnp.int32)])
    hit = (p[:, None] == window_index[None, :]) & valid[None, :]
    latest = jnp.max(jnp.where(hit, p[None, :], 0), axis=1)
    some = jnp.max(hit.astype(jnp.int32), axis=1)
    pairs = jnp.stack([chunk, window_index, base, same, latest, some]).astype(jnp.int32)

    vmem = pl.BlockSpec(memory_space=pltpu.VMEM)
    dma = pltpu.SemaphoreType.DMA
    out = pl.pallas_call(
        kernel,
        out_shape=jax.ShapeDtypeStruct(increment.shape, F32),
        in_specs=[vmem] * 10 + [pl.BlockSpec(memory_space=pltpu.SMEM)],
        out_specs=vmem,
        scratch_shapes=[
            pltpu.VMEM((4, ROWS + 2, LV, NX), F32),
            pltpu.VMEM((ROWS + 2, LEVB, NX), F32),
            pltpu.VMEM((5, ROWS, LEVB, NX), F32),
            pltpu.VMEM((4, ROWS, LEVB, NX), F32),
            pltpu.VMEM((ROWS, LV, NX), F32),
            pltpu.VMEM((2, 2, LV, NX), BF16),
            pltpu.VMEM((2, 2, LV + 16, LV), BF16),
            pltpu.VMEM((4, 2, VARS * ROWS, NX), F32),
            pltpu.VMEM((4, 3, VARS * ROWS, NX), F32),
            pltpu.VMEM((4, 8, 128), F32),
            pltpu.VMEM((CHUNKS, LV, CHUNK), F32),
            pltpu.VMEM((WINDOWS, 2 * LV, WIDE), BF16),
            pltpu.VMEM((PAIRS, WIDE, CHUNK), BF16),
            pltpu.VMEM((PAIRS, 1, CHUNK), F32),
            pltpu.VMEM((3, PAIRS, 1, CHUNK), F32),
            pltpu.VMEM((PAIRS, LV, WIDE), F32),
            dma((4, 2)), dma((4, 2)), dma((2,)), dma((2,)), dma((3,)), dma((3,)),
            dma((4, 3, 2)), dma((4, 3, 2)), dma((3,)), dma((3,)),
        ],
        compiler_params=pltpu.CompilerParams(
            collective_id=0, has_side_effects=True, vmem_limit_bytes=56 * 1024 * 1024),
    )(
        increment, courant_x, courant_y, mats, cols, coef, table,
        cell.reshape(CHUNKS, 1, CHUNK), blk.reshape(CHUNKS, 1, CHUNK), weight.reshape(CHUNKS, 1, CHUNK), pairs,
    )
    return out


def solution(mesh):
    return jax.shard_map(
        shards,
        mesh=mesh,
        in_specs=(
            P("band", None, "tile", None),
            P("band", "tile", None),
            P("band", "tile", None),
            P(None, "band", None),
            P(),
            P("band", None, None),
            P("tile", None),
            P("tile", None),
            P("tile", None),
            P("tile", None),
        ),
        out_specs=P("band", None, "tile", None),
        check_vma=False,
    )
```

```python
import functools

import jax
import jax.numpy as jnp
from jax import lax
from jax.experimental import pallas as pl
from jax.experimental.pallas import tpu as pltpu
from jax.sharding import PartitionSpec as P

MESH = pl.DeviceIdType.MESH
VARS = 5
LEVB = 16
LV = VARS * LEVB
ROWS = 8
NX = 768
BANDS = 4
TILES = 32
CHUNK = 256
CHUNKS = 32
WIDE = 256
WINDOWS = 24
PAIRS = 56
NBLK = 64
ORDER = (1, 2, 3, 4, 5, 6, 0, 7)
SPLIT = 24
F32 = jnp.float32
BF16 = jnp.bfloat16


def halves(value):
    high = value.astype(BF16)
    low = (value - high.astype(F32)).astype(BF16)
    return high, low


def mm(a, b):
    return jnp.dot(a, b, preferred_element_type=F32)


def wide(value):
    return jnp.concatenate([value] * (NX // 128), axis=1)


def sort_pairs(keys, payload):
    shape = keys.shape
    slab, sub, lane = (lax.broadcasted_iota(jnp.int32, shape, axis) for axis in range(3))
    place = lane * 64 + sub * 8 + slab
    for k in range(1, 14):
        for j in range(k - 1, -1, -1):
            distance = 1 << j
            bit, block = (place >> j) & 1, (place >> k) & 1
            flip = bit != block
            if j < 3:
                def partner(x):
                    parts = x.reshape(8 >> (j + 1), 2, distance, 8, 128)
                    return jnp.concatenate([parts[:, 1:], parts[:, :1]], axis=1).reshape(shape)
            else:
                axis, step, size = (1, distance >> 3, 8) if j < 6 else (2, distance >> 6, 128)

                def partner(x):
                    if 2 * step == size:
                        return pltpu.roll(x, step, axis)
                    return jnp.where(bit == 1, pltpu.roll(x, step, axis), pltpu.roll(x, size - step, axis))
            other, other_payload = partner(keys), partner(payload)
            take = jnp.where(flip, (keys < other).astype(jnp.int32), (keys > other).astype(jnp.int32)) == 1
            keys = jnp.where(take, other, keys)
            payload = jnp.where(take, other_payload, payload)
    return keys, payload


def kernel(
    inc_ref, cx_ref, cy_ref, inv_ref, prof_ref, column_ref, block_ref, weight_ref, coupling_ref, count_ref,
    out_ref,
    field, cyh, co, adj, local, stack, mext, gm, cols, tab, edges, recv, coefs, wbuf, wrow, turn, turn_key, keyr, wgtr, pairv,
    ps, xs, onehot, val, valr, acc, finals, pair_ref,
    halo_s, halo_r, cy_s, cy_r, cf_s, cf_r, ed_s, ed_r, va_s, va_r, wt_s, wt_r, pair_sem, out_sem,
):
    band = lax.axis_index("band")
    tile = lax.axis_index("tile")
    north = lax.rem(tile + 1, TILES)
    south = lax.rem(tile + TILES - 1, TILES)
    partner = [lax.rem(band + o, BANDS) for o in (1, 2, 3)]

    barrier = pltpu.get_barrier_semaphore()
    for o in range(1, TILES):
        pl.semaphore_signal(
            barrier, inc=1, device_id={"tile": lax.rem(tile + o, TILES)}, device_id_type=MESH)
    for p in partner:
        pl.semaphore_signal(barrier, inc=1, device_id={"band": p}, device_id_type=MESH)
    pl.semaphore_wait(barrier, TILES + BANDS - 2)

    sent = []

    def halo(buffer, send, receive):
        up = pltpu.make_async_remote_copy(
            buffer.at[ROWS], buffer.at[0], send.at[0], receive.at[0],
            device_id={"tile": north}, device_id_type=MESH)
        down = pltpu.make_async_remote_copy(
            buffer.at[1], buffer.at[ROWS + 1], send.at[1], receive.at[1],
            device_id={"tile": south}, device_id_type=MESH)
        up.start()
        down.start()
        sent.extend([up, down])
        return up, down

    def band_copy(source, target, send, receive, o):
        copy = pltpu.make_async_remote_copy(
            source, target, send, receive, device_id={"band": partner[o]}, device_id_type=MESH)
        copy.start()
        sent.append(copy)
        return copy

    for v in range(VARS):
        turned = jnp.swapaxes(inc_ref[:, v], 0, 1)
        field[0, 1:ROWS + 1, LEVB * v:LEVB * v + LEVB, :] = turned
    halo1 = halo(field.at[0], halo_s.at[0], halo_r.at[0])
    gm[...] = jnp.zeros((2, 128, 128), F32)
    for v in range(VARS):
        rows = slice(LEVB * v, LEVB * v + LEVB)
        gm[0, rows, rows] = inv_ref[v]
        tab[rows, :] = prof_ref[:, v, :]
    gm[1] = gm[0].T
    row_lane = lax.broadcasted_iota(jnp.int32, (8, 128), 1)

    def at_lanes(offset, factors):
        total = jnp.zeros((8, 128), F32)
        for v in range(VARS):
            total = total + jnp.where(row_lane == LEVB * v + offset, factors[v], 0.0)
        return total

    def rows_of(kind, offset):
        rows = [gm[kind, LEVB * v + offset:LEVB * v + offset + 1, :] for v in range(VARS)]
        if kind == 1:
            rows = [coupling_ref[v] * rows[v] for v in range(VARS)]
        return jnp.concatenate(rows + [jnp.zeros((3, 128), F32)], axis=0)

    ones = [1.0] * VARS
    scales = [coupling_ref[v] for v in range(VARS)]
    scale_first, scale_last = at_lanes(0, scales), at_lanes(LEVB - 1, scales)
    one_first, one_last = at_lanes(0, ones), at_lanes(LEVB - 1, ones)
    lasts = [rows_of(kind, LEVB - 1) for kind in range(2)]
    firsts = [rows_of(kind, 0) for kind in range(2)]

    def across(value, weight):
        return jnp.broadcast_to(jnp.sum(value * weight[0:1], axis=1, keepdims=True), (value.shape[0], 128))

    coefs[0, 0] = across(firsts[0], scale_first)
    coefs[0, 1] = across(lasts[0], scale_first)
    coefs[0, 2] = across(firsts[0], scale_last)
    cf_copies = [
        band_copy(coefs.at[0], coefs.at[o + 1], cf_s.at[o], cf_r.at[o], o) for o in range(3)
    ]
    cols[0, 0] = across(gm[0, :LV], scale_first)
    cols[0, 1] = across(gm[0, :LV], scale_last)
    cols[1, 0] = across(gm[1, :LV], one_first)
    cols[1, 1] = across(gm[1, :LV], one_last)

    wt_copies = []
    for o in range(1, TILES):
        target = lax.rem(tile + o, TILES)
        copy = pltpu.make_async_remote_copy(
            weight_ref.at[pl.ds(2 * target, 2)], wbuf.at[pl.ds(2 * tile, 2)], wt_s.at[o - 1], wt_r.at[o - 1],
            device_id={"tile": target}, device_id_type=MESH)
        copy.start()
        sent.append(copy)
        wt_copies.append(copy)
    cyh[1:ROWS + 1] = jnp.swapaxes(cy_ref[...], 0, 1)
    halo_cy = halo(cyh, cy_s, cy_r)
    co[0] = jnp.swapaxes(cx_ref[...], 0, 1)

    lane = lax.broadcasted_iota(jnp.int32, (LEVB, NX), 1)
    for y in range(ROWS):
        cx = co[0, y]
        cy = cyh[y + 1]
        ax, bx = (jnp.abs(cx) + cx) * 0.5, (jnp.abs(cx) - cx) * 0.5
        ay, by = (jnp.abs(cy) + cy) * 0.5, (jnp.abs(cy) - cy) * 0.5
        co[0, y] = 1.0 - ax - bx - ay - by
        co[1, y] = jnp.where(lane == 0, 0.0, ax)
        co[2, y] = jnp.where(lane == NX - 1, 0.0, bx)
        if y == 0:
            ay = jnp.where(tile == 0, 0.0, ay)
        if y == ROWS - 1:
            by = jnp.where(tile == TILES - 1, 0.0, by)
        co[3, y] = ay
        co[4, y] = by
        adj[0, y] = jnp.where(lane == 0, 0.0, pltpu.roll(bx, 1, 1))
        adj[1, y] = jnp.where(lane == NX - 1, 0.0, pltpu.roll(ax, NX - 1, 1))

    for copy in cf_copies:
        copy.wait_recv()

    def of_band(lane_index):
        result = []
        for j in range(BANDS):
            total = jnp.zeros((8, 128), F32)
            for b in range(BANDS):
                entry = coefs[(b - j) % BANDS, lane_index]
                total = total + jnp.where(band == b, entry, 0.0)
            result.append(total)
        return result

    def select(values):
        total = jnp.zeros((8, 128), F32)
        for b in range(BANDS):
            total = total + jnp.where(band == b, values[b], 0.0)
        return total

    k0, k15, g0 = of_band(0), of_band(1), of_band(2)
    zero = jnp.zeros((8, 128), F32)

    def chain(a, g):
        e = [zero] * (BANDS + 1)
        for j in range(BANDS - 1, -1, -1):
            e[j] = k0[j] + g[j] * e[j + 1] * a[j]
        into_first = select([g[b] * e[b + 1] for b in range(BANDS)])
        own = select([e[b + 1] for b in range(BANDS)])
        low, high = [], []
        for o in (1, 2, 3):
            t_list, s_list = [], []
            for b in range(BANDS):
                j = (b - o) % BANDS
                factor = zero + 1.0
                if j < b:
                    for k in range(j + 1, b):
                        factor = factor * a[k]
                    t_list.append(factor)
                    s_list.append(e[b + 1] * a[b] * factor)
                else:
                    for k in range(b + 1, j):
                        factor = factor * g[k]
                    t_list.append(zero)
                    s_list.append(factor)
            low.append(select(t_list))
            high.append(select(s_list))
        return into_first, own, low, high

    chains = (chain(k15, g0), chain(g0, k15))
    for kind in range(2):
        first = firsts[kind] + chains[kind][0] * lasts[kind]
        matrix = jnp.concatenate([gm[kind, :LV, :], lasts[kind], first], axis=0)[:, :LV]
        high, low = halves(matrix)
        mext[kind] = jnp.concatenate([high, high, low], axis=1)

    def stencil(src, y, v, kind):
        rows = slice(LEVB * v, LEVB * v + LEVB)
        f = field[src, y + 1, rows, :]
        west, east = pltpu.roll(f, 1, 1), pltpu.roll(f, NX - 1, 1)
        if kind == 0:
            cw, ce, cs, cn = (co[i, y] for i in (1, 2, 3, 4))
        else:
            cw, ce, cs, cn = adj[0, y], adj[1, y], adj[2, y], adj[3, y]
        return (
            co[0, y] * f + cw * west + ce * east
            + cs * field[src, y, rows, :] + cn * field[src, y + 2, rows, :]
        )

    def solve(stage, kind, row_value, before_last, store_row, after_edges, gap=None):
        copies = []
        for k, y in enumerate(ORDER):
            if k == 6:
                before_last()
            for v in range(VARS):
                high, low = halves(row_value(y, v))
                rows = slice(LEVB * v, LEVB * v + LEVB)
                stack[k % 2, rows, :] = high
                stack[k % 2, LV + LEVB * v:LV + LEVB * v + LEVB, :] = low
                stack[k % 2, 2 * LV + LEVB * v:2 * LV + LEVB * v + LEVB, :] = high
            result = mm(mext[kind], stack[k % 2])
            local[y] = result[:LV]
            edges[stage, 0, VARS * k:VARS * k + VARS, :] = result[LV:LV + VARS]
            edges[stage, 1, VARS * k:VARS * k + VARS, :] = result[LV + 8:LV + 8 + VARS]
            for part, (at, lo, hi) in enumerate(((4, 0, SPLIT), (7, SPLIT, VARS * ROWS))):
                if k == at:
                    for o in range(3):
                        above = (band + o + 1) // BANDS
                        copies.append(band_copy(
                            edges.at[stage, above, lo:hi], recv.at[stage, o, lo:hi],
                            ed_s.at[stage, o, part], ed_r.at[stage, o, part], o))
        if gap is not None:
            gap()
        for copy in copies:
            copy.wait_recv()
        _, own, low_c, high_c = chains[kind]
        for y in (0, 7, 1, 2, 3, 4, 5, 6):
            k = ORDER.index(y)
            span = slice(VARS * k, VARS * k + VARS)
            t = jnp.zeros((VARS, NX), F32)
            s = wide(own[:VARS]) * edges[stage, 0, span, :]
            for o in range(3):
                got = recv[stage, o, span, :]
                t = t + wide(low_c[o][:VARS]) * got
                s = s + wide(high_c[o][:VARS]) * got
            for v in range(VARS):
                rows = slice(LEVB * v, LEVB * v + LEVB)
                left, right = wide(cols[kind, 0, rows, :]), wide(cols[kind, 1, rows, :])
                store_row(y, v, local[y, rows, :] + left * t[v:v + 1] + right * s[v:v + 1])
            if y == 7:
                after_edges()

    pending = {}

    def wait_halo(copies):
        for copy in copies:
            copy.wait_recv()

    def into_field(index):
        def store(y, v, value):
            field[index, y + 1, LEVB * v:LEVB * v + LEVB, :] = value
        return store

    def send_field(index):
        def send():
            pending[index] = halo(field.at[index], halo_s.at[index], halo_r.at[index])
        return send

    def store_state(y, v, value):
        high, low = halves(value)
        for j in range(3):
            cols = slice(WIDE * j, WIDE * j + WIDE)
            xs[3 * y + j, LEVB * v:LEVB * v + LEVB, :] = high[:, cols]
            xs[3 * y + j, LV + LEVB * v:LV + LEVB * v + LEVB, :] = low[:, cols]

    def sort_slots():
        for copy in wt_copies:
            copy.wait_recv()
        own = pl.ds(2 * tile, 2)
        wbuf[own] = weight_ref[own]
        slot = lax.broadcasted_iota(jnp.int32, (1, 128), 1)
        for r in range(64):
            live = slot < count_ref[0, r // 2] - 128 * (r % 2)
            wrow[r:r + 1, :] = jnp.where(live, wbuf[r], 0.0)
        keys = (column_ref[...] * NBLK + block_ref[...]).reshape(8, 8, 128)
        keys, weights = sort_pairs(keys, wrow[...].reshape(8, 8, 128))
        turn_key[0:64, :] = keys.reshape(64, 128)
        turn_key[64:128, :] = jnp.zeros((64, 128), jnp.int32)
        turn_key[...] = turn_key[...].T
        turn[0:64, :] = weights.reshape(64, 128)
        turn[64:128, :] = jnp.zeros((64, 128), F32)
        turn[...] = turn[...].T

        def rows_of_chunks(ref):
            return jnp.concatenate(
                [ref[pl.ds(q, CHUNKS, stride=4), :][:, :64] for q in range(4)], axis=1)

        rows, weights = rows_of_chunks(turn_key), rows_of_chunks(turn)
        for c in range(CHUNKS):
            keyr[c] = rows[c:c + 1]
            wgtr[c] = weights[c:c + 1]
        first = jnp.broadcast_to(rows[:, 0:1] // (NBLK * WIDE), (CHUNKS, 128))
        last = jnp.broadcast_to(rows[:, CHUNK - 1:CHUNK] // (NBLK * WIDE), (CHUNKS, 128))
        number = last - first + 1
        sub = lax.broadcasted_iota(jnp.int32, (CHUNKS, 128), 0)
        p = lax.broadcasted_iota(jnp.int32, (CHUNKS, 128), 1)
        upto = number
        for d in (1, 2, 4, 8, 16):
            upto = upto + jnp.where(sub >= d, pltpu.roll(upto, d, 0), 0)
        start = upto - number

        def down(value):
            return jnp.sum(value, axis=0, keepdims=True)

        chunk = jnp.clip(down(jnp.where(start <= p, 1, 0)) - 1, 0, CHUNKS - 1)
        window = down(jnp.where(sub == chunk, first - start + p, 0))
        valid = p[0:1] < upto[CHUNKS - 1:CHUNKS]
        index = jnp.clip(jnp.where(valid, window, WINDOWS - 1), 0, WINDOWS - 1)
        base = jnp.where(valid, window * WIDE, -(1 << 20))
        same = jnp.where((p[0:1] > 0) & (index == pltpu.roll(index, 1, 1)), 1, 0)
        latest = jnp.clip(down(jnp.clip(p - first + 1, 0, number)) - 1, 0, PAIRS - 1)
        some = jnp.minimum(down(jnp.where((first <= p) & (p <= last), 1, 0)), 1)
        zeros = jnp.zeros((2, 128), jnp.int32)
        pairv[...] = jnp.concatenate([chunk, index, base, same, latest, some, zeros], axis=0)
        copy = pltpu.make_async_copy(pairv, pair_ref, pair_sem)
        copy.start()
        copy.wait()

    def pick_slots():
        profiles = jnp.concatenate(halves(tab[...]), axis=0)
        block_iota = lax.broadcasted_iota(jnp.int32, (NBLK, CHUNK), 0)
        cell_iota = lax.broadcasted_iota(jnp.int32, (WIDE, CHUNK), 0)

        def pick_profiles(i, carry):
            for u in range(4):
                c = 4 * i + u
                picked = mm(profiles, (block_iota == keyr[c] % NBLK).astype(BF16))
                ps[c] = picked[:LV] + picked[LV:]
            return carry

        lax.fori_loop(0, CHUNKS // 4, pick_profiles, 0)

        def pick_cells(i, carry):
            for u in range(4):
                p = 4 * i + u
                onehot[p] = (cell_iota == keyr[pair_ref[0, p]] // NBLK - pair_ref[2, p]).astype(BF16)
            return carry

        lax.fori_loop(0, PAIRS // 4, pick_cells, 0)

    solve(0, 0, lambda y, v: stencil(0, y, v, 0), lambda: wait_halo(halo1), into_field(1), send_field(1), sort_slots)
    solve(1, 0, lambda y, v: stencil(1, y, v, 0), lambda: wait_halo(pending[1]), store_state, lambda: None, pick_slots)

    def observe(i, carry):
        for u in range(4):
            p = 4 * i + u
            picked = mm(xs[pair_ref[1, p]], onehot[p])
            product = (picked[:LV] + picked[LV:]) * ps[pair_ref[0, p]]
            val[p] = jnp.sum(product, axis=0, keepdims=True)
        return carry

    lax.fori_loop(0, PAIRS // 4, observe, 0)
    copies = [band_copy(val, valr.at[o], va_s.at[o], va_r.at[o], o) for o in range(3)]

    wait_halo(halo_cy)
    for y in range(ROWS):
        below, above = cyh[y], cyh[y + 2]
        by = (jnp.abs(below) - below) * 0.5
        ay = (jnp.abs(above) + above) * 0.5
        if y == 0:
            by = jnp.where(tile == 0, 0.0, by)
        if y == ROWS - 1:
            ay = jnp.where(tile == TILES - 1, 0.0, ay)
        adj[2, y] = by
        adj[3, y] = ay
    for copy in copies:
        copy.wait_recv()

    def spread(i, before):
        for u in range(4):
            p = 4 * i + u
            c = pair_ref[0, p]
            values = (val[p] + valr[0, p]) + (valr[1, p] + valr[2, p])
            high, low = halves(ps[c] * (values * wgtr[c]))
            both = jnp.concatenate([high, low], axis=0)
            added = lax.dot_general(
                both, onehot[p], (((1,), (1,)), ((), ())), preferred_element_type=F32)
            before = before * pair_ref[3, p].astype(F32) + (added[:LV] + added[LV:])
            acc[p] = before
        return before

    lax.fori_loop(0, PAIRS // 4, spread, jnp.zeros((LV, WIDE), F32))

    def gradient(y, v):
        parts = []
        for j in range(3):
            w = 3 * y + j
            some = pair_ref[5, w].astype(F32)
            parts.append(acc[pair_ref[4, w], LEVB * v:LEVB * v + LEVB, :] * some)
        return jnp.concatenate(parts, axis=1)

    solve(2, 1, gradient, lambda: None, into_field(2), send_field(2))
    solve(3, 1, lambda y, v: stencil(2, y, v, 1), lambda: wait_halo(pending[2]), into_field(3), send_field(3))

    def finish(y, v):
        rows = slice(LEVB * v, LEVB * v + LEVB)
        local[y, rows, :] = stencil(3, y, v, 1) + field[0, y + 1, rows, :]

    for y in ORDER[:6]:
        for v in range(VARS):
            finish(y, v)
    wait_halo(pending[3])
    outs = []
    for v in range(VARS):
        for y in ORDER[6:]:
            finish(y, v)
        out_stage = finals.at[v]
        out_stage[...] = jnp.swapaxes(local[:, LEVB * v:LEVB * v + LEVB, :], 0, 1)
        outs.append(pltpu.make_async_copy(out_stage, out_ref.at[:, v], out_sem.at[v]))
        outs[-1].start()
    for copy in outs:
        copy.wait()
    for copy in sent:
        copy.wait_send()


def shards(
    increment, courant_x, courant_y, level_inverse, coupling, profile, send_column, send_block, send_count, obs_weight,
):
    vmem = pl.BlockSpec(memory_space=pltpu.VMEM)
    smem = pl.BlockSpec(memory_space=pltpu.SMEM)
    dma = pltpu.SemaphoreType.DMA
    return pl.pallas_call(
        kernel,
        out_shape=jax.ShapeDtypeStruct(increment.shape, F32),
        in_specs=[vmem] * 8 + [smem] * 2,
        out_specs=pl.BlockSpec(memory_space=pl.ANY),
        scratch_shapes=[
            pltpu.VMEM((4, ROWS + 2, LV, NX), F32),
            pltpu.VMEM((ROWS + 2, LEVB, NX), F32),
            pltpu.VMEM((5, ROWS, LEVB, NX), F32),
            pltpu.VMEM((4, ROWS, LEVB, NX), F32),
            pltpu.VMEM((ROWS, LV, NX), F32),
            pltpu.VMEM((2, 3 * LV, NX), BF16),
            pltpu.VMEM((2, LV + 16, 3 * LV), BF16),
            pltpu.VMEM((2, 128, 128), F32),
            pltpu.VMEM((2, 2, LV, 128), F32),
            pltpu.VMEM((LV, NBLK), F32),
            pltpu.VMEM((4, 2, VARS * ROWS, NX), F32),
            pltpu.VMEM((4, 3, VARS * ROWS, NX), F32),
            pltpu.VMEM((4, 3, 8, 128), F32),
            pltpu.VMEM((64, 1, 128), F32),
            pltpu.VMEM((64, 128), F32),
            pltpu.VMEM((128, 128), F32),
            pltpu.VMEM((128, 128), jnp.int32),
            pltpu.VMEM((CHUNKS, 1, CHUNK), jnp.int32),
            pltpu.VMEM((CHUNKS, 1, CHUNK), F32),
            pltpu.VMEM((8, 128), jnp.int32),
            pltpu.VMEM((CHUNKS, LV, CHUNK), F32),
            pltpu.VMEM((WINDOWS, 2 * LV, WIDE), BF16),
            pltpu.VMEM((PAIRS, WIDE, CHUNK), BF16),
            pltpu.VMEM((PAIRS, 1, CHUNK), F32),
            pltpu.VMEM((3, PAIRS, 1, CHUNK), F32),
            pltpu.VMEM((PAIRS, LV, WIDE), F32),
            pltpu.VMEM((VARS, LEVB, ROWS, NX), F32),
            pltpu.SMEM((8, 128), jnp.int32),
            dma((4, 2)), dma((4, 2)), dma((2,)), dma((2,)), dma((3,)), dma((3,)),
            dma((4, 3, 2)), dma((4, 3, 2)), dma((3,)), dma((3,)), dma((TILES - 1,)), dma((TILES - 1,)),
            dma, dma((VARS,)),
        ],
        compiler_params=pltpu.CompilerParams(
            collective_id=0, has_side_effects=True, vmem_limit_bytes=56 * 1024 * 1024),
    )(
        increment, courant_x, courant_y, level_inverse, profile,
        send_column.reshape(64, 128), send_block.reshape(64, 128), obs_weight.reshape(64, 1, 128),
        coupling, send_count,
    )


def solution(mesh):
    return jax.shard_map(
        shards,
        mesh=mesh,
        in_specs=(
            P("band", None, "tile", None),
            P("band", "tile", None),
            P("band", "tile", None),
            P(None, "band", None),
            P(),
            P("band", None, None),
            P("tile", None),
            P("tile", None),
            P("tile", None),
            P("tile", None),
        ),
        out_specs=P("band", None, "tile", None),
        check_vma=False,
    )
```

```python
import functools

import jax
import jax.numpy as jnp
from jax import lax
from jax.experimental import pallas as pl
from jax.experimental.pallas import tpu as pltpu
from jax.sharding import PartitionSpec as P

MESH = pl.DeviceIdType.MESH
VARS = 5
LEVB = 16
LV = VARS * LEVB
ROWS = 8
NX = 768
BANDS = 4
TILES = 32
CHUNK = 256
CHUNKS = 32
WIDE = 256
WINDOWS = 24
PAIRS = 56
NBLK = 64
INNER_FIRST = (1, 2, 3, 4, 5, 6, 0, 7)
OUTER_FIRST = (0, 7, 1, 2, 3, 4, 5, 6)
SPLIT = 24
F32 = jnp.float32
BF16 = jnp.bfloat16


def halves(value):
    high = value.astype(BF16)
    low = (value - high.astype(F32)).astype(BF16)
    return high, low


def mm(a, b):
    return jnp.dot(a, b, preferred_element_type=F32)


def wide(value):
    return jnp.concatenate([value] * (NX // 128), axis=1)


def sort_pairs(keys, payload):
    shape = keys.shape
    slab, sub, lane = (lax.broadcasted_iota(jnp.int32, shape, axis) for axis in range(3))
    place = lane * 64 + sub * 8 + slab
    for k in range(1, 14):
        for j in range(k - 1, -1, -1):
            distance = 1 << j
            bit, block = (place >> j) & 1, (place >> k) & 1
            flip = bit != block
            if j < 3:
                def partner(x):
                    parts = x.reshape(8 >> (j + 1), 2, distance, 8, 128)
                    return jnp.concatenate([parts[:, 1:], parts[:, :1]], axis=1).reshape(shape)
            else:
                axis, step, size = (1, distance >> 3, 8) if j < 6 else (2, distance >> 6, 128)

                def partner(x):
                    if 2 * step == size:
                        return pltpu.roll(x, step, axis)
                    return jnp.where(bit == 1, pltpu.roll(x, step, axis), pltpu.roll(x, size - step, axis))
            other, other_payload = partner(keys), partner(payload)
            take = jnp.where(flip, (keys < other).astype(jnp.int32), (keys > other).astype(jnp.int32)) == 1
            keys = jnp.where(take, other, keys)
            payload = jnp.where(take, other_payload, payload)
    return keys, payload


def kernel(
    inc_ref, cx_ref, cy_ref, inv_ref, prof_ref, column_ref, block_ref, weight_ref, coupling_ref, count_ref,
    out_ref,
    field, cyh, co, adj, local, stack, mext, gm, cols, tab, edges, recv, beside, corner, coefs, wbuf, wrow, turn, turn_key, keyr, wgtr, pairv,
    ps, xs, onehot, val, valr, acc, finals, pair_ref,
    first_s, first_r, halo_s, halo_r, diag_s, diag_r, cy_s, cy_r, cf_s, cf_r, ed_s, ed_r, va_s, va_r, wt_s, wt_r, pair_sem, out_sem,
):
    band = lax.axis_index("band")
    tile = lax.axis_index("tile")
    north = lax.rem(tile + 1, TILES)
    south = lax.rem(tile + TILES - 1, TILES)
    partner = [lax.rem(band + o, BANDS) for o in (1, 2, 3)]

    barrier = pltpu.get_barrier_semaphore()
    for o in range(1, TILES):
        pl.semaphore_signal(
            barrier, inc=1, device_id={"tile": lax.rem(tile + o, TILES)}, device_id_type=MESH)
    for p in partner:
        pl.semaphore_signal(barrier, inc=1, device_id={"band": p}, device_id_type=MESH)
    for p in partner:
        for t in (north, south):
            pl.semaphore_signal(barrier, inc=1, device_id={"tile": t, "band": p}, device_id_type=MESH)

    sent = []

    def halo(buffer, send, receive):
        up = pltpu.make_async_remote_copy(
            buffer.at[ROWS], buffer.at[0], send.at[0], receive.at[0],
            device_id={"tile": north}, device_id_type=MESH)
        down = pltpu.make_async_remote_copy(
            buffer.at[1], buffer.at[ROWS + 1], send.at[1], receive.at[1],
            device_id={"tile": south}, device_id_type=MESH)
        up.start()
        down.start()
        sent.extend([up, down])
        return up, down

    def band_copy(source, target, send, receive, o):
        copy = pltpu.make_async_remote_copy(
            source, target, send, receive, device_id={"band": partner[o]}, device_id_type=MESH)
        copy.start()
        sent.append(copy)
        return copy

    for v in range(VARS):
        turned = jnp.swapaxes(inc_ref[:, v], 0, 1)
        field[0, 1:ROWS + 1, LEVB * v:LEVB * v + LEVB, :] = turned
    gm[...] = jnp.zeros((2, 128, 128), F32)
    for v in range(VARS):
        rows = slice(LEVB * v, LEVB * v + LEVB)
        gm[0, rows, rows] = inv_ref[v]
        tab[rows, :] = prof_ref[v]
    gm[1] = gm[0].T
    row_lane = lax.broadcasted_iota(jnp.int32, (8, 128), 1)

    def at_lanes(offset, factors):
        total = jnp.zeros((8, 128), F32)
        for v in range(VARS):
            total = total + jnp.where(row_lane == LEVB * v + offset, factors[v], 0.0)
        return total

    def rows_of(kind, offset):
        rows = [gm[kind, LEVB * v + offset:LEVB * v + offset + 1, :] for v in range(VARS)]
        if kind == 1:
            rows = [coupling_ref[v] * rows[v] for v in range(VARS)]
        return jnp.concatenate(rows + [jnp.zeros((3, 128), F32)], axis=0)

    ones = [1.0] * VARS
    scales = [coupling_ref[v] for v in range(VARS)]
    scale_first, scale_last = at_lanes(0, scales), at_lanes(LEVB - 1, scales)
    one_first, one_last = at_lanes(0, ones), at_lanes(LEVB - 1, ones)
    lasts = [rows_of(kind, LEVB - 1) for kind in range(2)]
    firsts = [rows_of(kind, 0) for kind in range(2)]

    def across(value, weight):
        return jnp.broadcast_to(jnp.sum(value * weight[0:1], axis=1, keepdims=True), (value.shape[0], 128))

    coefs[0, 0] = across(firsts[0], scale_first)
    coefs[0, 1] = across(lasts[0], scale_first)
    coefs[0, 2] = across(firsts[0], scale_last)
    pl.semaphore_wait(barrier, TILES + BANDS - 2 + 2 * (BANDS - 1))
    halo1 = halo(field.at[0], first_s, first_r)
    cf_copies = [
        band_copy(coefs.at[0], coefs.at[o + 1], cf_s.at[o], cf_r.at[o], o) for o in range(3)
    ]
    cols[0, 0] = across(gm[0, :LV], scale_first)
    cols[0, 1] = across(gm[0, :LV], scale_last)
    cols[1, 0] = across(gm[1, :LV], one_first)
    cols[1, 1] = across(gm[1, :LV], one_last)

    wt_copies = []
    for o in range(1, TILES):
        target = lax.rem(tile + o, TILES)
        copy = pltpu.make_async_remote_copy(
            weight_ref.at[pl.ds(2 * target, 2)], wbuf.at[pl.ds(2 * tile, 2)], wt_s.at[o - 1], wt_r.at[o - 1],
            device_id={"tile": target}, device_id_type=MESH)
        copy.start()
        sent.append(copy)
        wt_copies.append(copy)
    cyh[1:ROWS + 1] = jnp.swapaxes(cy_ref[...], 0, 1)
    halo_cy = halo(cyh, cy_s, cy_r)
    co[0] = jnp.swapaxes(cx_ref[...], 0, 1)

    lane = lax.broadcasted_iota(jnp.int32, (LEVB, NX), 1)
    for y in range(ROWS):
        cx = co[0, y]
        cy = cyh[y + 1]
        ax, bx = (jnp.abs(cx) + cx) * 0.5, (jnp.abs(cx) - cx) * 0.5
        ay, by = (jnp.abs(cy) + cy) * 0.5, (jnp.abs(cy) - cy) * 0.5
        co[0, y] = 1.0 - ax - bx - ay - by
        co[1, y] = jnp.where(lane == 0, 0.0, ax)
        co[2, y] = jnp.where(lane == NX - 1, 0.0, bx)
        if y == 0:
            ay = jnp.where(tile == 0, 0.0, ay)
        if y == ROWS - 1:
            by = jnp.where(tile == TILES - 1, 0.0, by)
        co[3, y] = ay
        co[4, y] = by
        adj[0, y] = jnp.where(lane == 0, 0.0, pltpu.roll(bx, 1, 1))
        adj[1, y] = jnp.where(lane == NX - 1, 0.0, pltpu.roll(ax, NX - 1, 1))

    for copy in cf_copies:
        copy.wait_recv()

    def of_band(lane_index):
        result = []
        for j in range(BANDS):
            total = jnp.zeros((8, 128), F32)
            for b in range(BANDS):
                entry = coefs[(b - j) % BANDS, lane_index]
                total = total + jnp.where(band == b, entry, 0.0)
            result.append(total)
        return result

    def select(values):
        total = jnp.zeros((8, 128), F32)
        for b in range(BANDS):
            total = total + jnp.where(band == b, values[b], 0.0)
        return total

    k0, k15, g0 = of_band(0), of_band(1), of_band(2)
    zero = jnp.zeros((8, 128), F32)

    def chain(a, g):
        e = [zero] * (BANDS + 1)
        for j in range(BANDS - 1, -1, -1):
            e[j] = k0[j] + g[j] * e[j + 1] * a[j]
        into_first = select([g[b] * e[b + 1] for b in range(BANDS)])
        own = select([e[b + 1] for b in range(BANDS)])
        low, high = [], []
        for o in (1, 2, 3):
            t_list, s_list = [], []
            for b in range(BANDS):
                j = (b - o) % BANDS
                factor = zero + 1.0
                if j < b:
                    for k in range(j + 1, b):
                        factor = factor * a[k]
                    t_list.append(factor)
                    s_list.append(e[b + 1] * a[b] * factor)
                else:
                    for k in range(b + 1, j):
                        factor = factor * g[k]
                    t_list.append(zero)
                    s_list.append(factor)
            low.append(select(t_list))
            high.append(select(s_list))
        return into_first, own, low, high

    chains = (chain(k15, g0), chain(g0, k15))
    for kind in range(2):
        first = firsts[kind] + chains[kind][0] * lasts[kind]
        matrix = jnp.concatenate([gm[kind, :LV, :], lasts[kind], first], axis=0)[:, :LV]
        high, low = halves(matrix)
        mext[kind] = jnp.concatenate([high, high, low], axis=1)

    def stencil(src, y, v, kind):
        rows = slice(LEVB * v, LEVB * v + LEVB)
        f = field[src, y + 1, rows, :]
        west, east = pltpu.roll(f, 1, 1), pltpu.roll(f, NX - 1, 1)
        if kind == 0:
            cw, ce, cs, cn = (co[i, y] for i in (1, 2, 3, 4))
        else:
            cw, ce, cs, cn = adj[0, y], adj[1, y], adj[2, y], adj[3, y]
        return (
            co[0, y] * f + cw * west + ce * east
            + cs * field[src, y, rows, :] + cn * field[src, y + 2, rows, :]
        )

    def solve(stage, kind, order, row_value, store_row, slot=None, before=None, gap=None):
        copies, halos = [], []
        for k, y in enumerate(order):
            if k == 6 and before is not None:
                before()
            for v in range(VARS):
                high, low = halves(row_value(y, v))
                rows = slice(LEVB * v, LEVB * v + LEVB)
                stack[k % 2, rows, :] = high
                stack[k % 2, LV + LEVB * v:LV + LEVB * v + LEVB, :] = low
                stack[k % 2, 2 * LV + LEVB * v:2 * LV + LEVB * v + LEVB, :] = high
            result = mm(mext[kind], stack[k % 2])
            local[stage, y] = result.reshape(12, 8, NX)
            edges[stage, 0, VARS * k:VARS * k + VARS, :] = result[LV:LV + VARS]
            edges[stage, 1, VARS * k:VARS * k + VARS, :] = result[LV + 8:LV + 8 + VARS]
            if slot is not None and y in (0, ROWS - 1):
                side, target = (1, south) if y == 0 else (0, north)
                copy = pltpu.make_async_remote_copy(
                    local.at[stage, y, 0:11], beside.at[slot, side], halo_s.at[slot, side], halo_r.at[slot, side],
                    device_id={"tile": target}, device_id_type=MESH)
                copy.start()
                halos.append(copy)
                for o in range(3):
                    above = (band + o + 1) // BANDS
                    copy = pltpu.make_async_remote_copy(
                        local.at[stage, y, 10 + above], corner.at[slot, side, o],
                        diag_s.at[slot, side, o], diag_r.at[slot, side, o],
                        device_id={"tile": target, "band": partner[o]}, device_id_type=MESH)
                    copy.start()
                    halos.append(copy)
            for part, (at, lo, hi) in enumerate(((4, 0, SPLIT), (7, SPLIT, VARS * ROWS))):
                if k == at:
                    for o in range(3):
                        above = (band + o + 1) // BANDS
                        copies.append(band_copy(
                            edges.at[stage, above, lo:hi], recv.at[stage, o, lo:hi],
                            ed_s.at[stage, o, part], ed_r.at[stage, o, part], o))
        sent.extend(halos)
        if gap is not None:
            gap()
        _, own, low_c, high_c = chains[kind]

        def complete(y, mine, got, parts):
            t = jnp.zeros((VARS, NX), F32)
            s = wide(own[:VARS]) * mine
            for o in range(3):
                t = t + wide(low_c[o][:VARS]) * got[o]
                s = s + wide(high_c[o][:VARS]) * got[o]
            for v in range(VARS):
                rows = slice(LEVB * v, LEVB * v + LEVB)
                left, right = wide(cols[kind, 0, rows, :]), wide(cols[kind, 1, rows, :])
                store_row(y, v, parts(v) + left * t[v:v + 1] + right * s[v:v + 1])

        for copy in copies:
            copy.wait_recv()
        for k, y in enumerate(order):
            span = slice(VARS * k, VARS * k + VARS)
            complete(
                y, edges[stage, 0, span, :], [recv[stage, o, span, :] for o in range(3)],
                lambda v: local[stage, y, 2 * v:2 * v + 2].reshape(LEVB, NX))
        for copy in halos:
            copy.wait_recv()
        if slot is not None:
            for side, y in ((0, -1), (1, ROWS)):
                complete(
                    y, beside[slot, side, 10][:VARS], [corner[slot, side, o][:VARS] for o in range(3)],
                    lambda v: beside[slot, side, 2 * v:2 * v + 2].reshape(LEVB, NX))

    def wait_halo(copies):
        for copy in copies:
            copy.wait_recv()

    def into_field(index):
        def store(y, v, value):
            field[index, y + 1, LEVB * v:LEVB * v + LEVB, :] = value
        return store

    def store_state(y, v, value):
        high, low = halves(value)
        for j in range(3):
            cols = slice(WIDE * j, WIDE * j + WIDE)
            xs[3 * y + j, LEVB * v:LEVB * v + LEVB, :] = high[:, cols]
            xs[3 * y + j, LV + LEVB * v:LV + LEVB * v + LEVB, :] = low[:, cols]

    def sort_slots():
        for copy in wt_copies:
            copy.wait_recv()
        own = pl.ds(2 * tile, 2)
        wbuf[own] = weight_ref[own]
        slot = lax.broadcasted_iota(jnp.int32, (1, 128), 1)
        for r in range(64):
            live = slot < count_ref[0, r // 2] - 128 * (r % 2)
            wrow[r:r + 1, :] = jnp.where(live, wbuf[r], 0.0)
        keys = (column_ref[...] * NBLK + block_ref[...]).reshape(8, 8, 128)
        keys, weights = sort_pairs(keys, wrow[...].reshape(8, 8, 128))
        turn_key[0:64, :] = keys.reshape(64, 128)
        turn_key[64:128, :] = jnp.zeros((64, 128), jnp.int32)
        turn_key[...] = turn_key[...].T
        turn[0:64, :] = weights.reshape(64, 128)
        turn[64:128, :] = jnp.zeros((64, 128), F32)
        turn[...] = turn[...].T

        def rows_of_chunks(ref):
            return jnp.concatenate(
                [ref[pl.ds(q, CHUNKS, stride=4), :][:, :64] for q in range(4)], axis=1)

        rows, weights = rows_of_chunks(turn_key), rows_of_chunks(turn)
        for c in range(CHUNKS):
            keyr[c] = rows[c:c + 1]
            wgtr[c] = weights[c:c + 1]
        first = jnp.broadcast_to(rows[:, 0:1] // (NBLK * WIDE), (CHUNKS, 128))
        last = jnp.broadcast_to(rows[:, CHUNK - 1:CHUNK] // (NBLK * WIDE), (CHUNKS, 128))
        number = last - first + 1
        sub = lax.broadcasted_iota(jnp.int32, (CHUNKS, 128), 0)
        p = lax.broadcasted_iota(jnp.int32, (CHUNKS, 128), 1)
        upto = number
        for d in (1, 2, 4, 8, 16):
            upto = upto + jnp.where(sub >= d, pltpu.roll(upto, d, 0), 0)
        start = upto - number

        def down(value):
            return jnp.sum(value, axis=0, keepdims=True)

        chunk = jnp.clip(down(jnp.where(start <= p, 1, 0)) - 1, 0, CHUNKS - 1)
        window = down(jnp.where(sub == chunk, first - start + p, 0))
        valid = p[0:1] < upto[CHUNKS - 1:CHUNKS]
        index = jnp.clip(jnp.where(valid, window, WINDOWS - 1), 0, WINDOWS - 1)
        base = jnp.where(valid, window * WIDE, -(1 << 20))
        same = jnp.where((p[0:1] > 0) & (index == pltpu.roll(index, 1, 1)), 1, 0)
        latest = jnp.clip(down(jnp.clip(p - first + 1, 0, number)) - 1, 0, PAIRS - 1)
        some = jnp.minimum(down(jnp.where((first <= p) & (p <= last), 1, 0)), 1)
        zeros = jnp.zeros((2, 128), jnp.int32)
        pairv[...] = jnp.concatenate([chunk, index, base, same, latest, some, zeros], axis=0)
        copy = pltpu.make_async_copy(pairv, pair_ref, pair_sem)
        copy.start()
        copy.wait()

    def pick_slots():
        profiles = jnp.concatenate(halves(tab[...]), axis=0)
        block_iota = lax.broadcasted_iota(jnp.int32, (NBLK, CHUNK), 0)
        cell_iota = lax.broadcasted_iota(jnp.int32, (WIDE, CHUNK), 0)

        def pick_profiles(i, carry):
            for u in range(4):
                c = 4 * i + u
                picked = mm(profiles, (block_iota == keyr[c] % NBLK).astype(BF16))
                ps[c] = picked[:LV] + picked[LV:]
            return carry

        lax.fori_loop(0, CHUNKS // 4, pick_profiles, 0)

        def pick_cells(i, carry):
            for u in range(4):
                p = 4 * i + u
                onehot[p] = (cell_iota == keyr[pair_ref[0, p]] // NBLK - pair_ref[2, p]).astype(BF16)
            return carry

        lax.fori_loop(0, PAIRS // 4, pick_cells, 0)

    solve(
        0, 0, INNER_FIRST, lambda y, v: stencil(0, y, v, 0), into_field(1), 0,
        before=lambda: wait_halo(halo1), gap=sort_slots)
    solve(1, 0, OUTER_FIRST, lambda y, v: stencil(1, y, v, 0), store_state, gap=pick_slots)

    def observe(i, carry):
        for u in range(4):
            p = 4 * i + u
            picked = mm(xs[pair_ref[1, p]], onehot[p])
            product = (picked[:LV] + picked[LV:]) * ps[pair_ref[0, p]]
            val[p] = jnp.sum(product, axis=0, keepdims=True)
        return carry

    lax.fori_loop(0, PAIRS // 4, observe, 0)
    copies = [band_copy(val, valr.at[o], va_s.at[o], va_r.at[o], o) for o in range(3)]

    wait_halo(halo_cy)
    for y in range(ROWS):
        below, above = cyh[y], cyh[y + 2]
        by = (jnp.abs(below) - below) * 0.5
        ay = (jnp.abs(above) + above) * 0.5
        if y == 0:
            by = jnp.where(tile == 0, 0.0, by)
        if y == ROWS - 1:
            ay = jnp.where(tile == TILES - 1, 0.0, ay)
        adj[2, y] = by
        adj[3, y] = ay
    for copy in copies:
        copy.wait_recv()

    def spread(i, before):
        for u in range(4):
            p = 4 * i + u
            c = pair_ref[0, p]
            values = (val[p] + valr[0, p]) + (valr[1, p] + valr[2, p])
            high, low = halves(ps[c] * (values * wgtr[c]))
            both = jnp.concatenate([high, low], axis=0)
            added = lax.dot_general(
                both, onehot[p], (((1,), (1,)), ((), ())), preferred_element_type=F32)
            before = before * pair_ref[3, p].astype(F32) + (added[:LV] + added[LV:])
            acc[p] = before
        return before

    lax.fori_loop(0, PAIRS // 4, spread, jnp.zeros((LV, WIDE), F32))

    def gradient(y, v):
        parts = []
        for j in range(3):
            w = 3 * y + j
            some = pair_ref[5, w].astype(F32)
            parts.append(acc[pair_ref[4, w], LEVB * v:LEVB * v + LEVB, :] * some)
        return jnp.concatenate(parts, axis=1)

    solve(2, 1, OUTER_FIRST, gradient, into_field(2), 1)
    solve(3, 1, OUTER_FIRST, lambda y, v: stencil(2, y, v, 1), into_field(3), 2)

    outs = []
    for v in range(VARS):
        rows = slice(LEVB * v, LEVB * v + LEVB)
        result = [stencil(3, y, v, 1) + field[0, y + 1, rows, :] for y in range(ROWS)]
        out_stage = finals.at[v]
        out_stage[...] = jnp.swapaxes(jnp.stack(result), 0, 1)
        outs.append(pltpu.make_async_copy(out_stage, out_ref.at[:, v], out_sem.at[v]))
        outs[-1].start()
    for copy in outs:
        copy.wait()
    for copy in sent:
        copy.wait_send()


def shards(
    increment, courant_x, courant_y, level_inverse, coupling, profile, send_column, send_block, send_count, obs_weight,
):
    vmem = pl.BlockSpec(memory_space=pltpu.VMEM)
    smem = pl.BlockSpec(memory_space=pltpu.SMEM)
    dma = pltpu.SemaphoreType.DMA
    return pl.pallas_call(
        kernel,
        out_shape=jax.ShapeDtypeStruct(increment.shape, F32),
        in_specs=[vmem] * 8 + [smem] * 2,
        out_specs=pl.BlockSpec(memory_space=pl.ANY),
        scratch_shapes=[
            pltpu.VMEM((4, ROWS + 2, LV, NX), F32),
            pltpu.VMEM((ROWS + 2, LEVB, NX), F32),
            pltpu.VMEM((5, ROWS, LEVB, NX), F32),
            pltpu.VMEM((4, ROWS, LEVB, NX), F32),
            pltpu.VMEM((4, ROWS, 12, 8, NX), F32),
            pltpu.VMEM((2, 3 * LV, NX), BF16),
            pltpu.VMEM((2, LV + 16, 3 * LV), BF16),
            pltpu.VMEM((2, 128, 128), F32),
            pltpu.VMEM((2, 2, LV, 128), F32),
            pltpu.VMEM((LV, NBLK), F32),
            pltpu.VMEM((4, 2, VARS * ROWS, NX), F32),
            pltpu.VMEM((4, 3, VARS * ROWS, NX), F32),
            pltpu.VMEM((3, 2, 11, 8, NX), F32),
            pltpu.VMEM((3, 2, 3, 8, NX), F32),
            pltpu.VMEM((4, 3, 8, 128), F32),
            pltpu.VMEM((64, 1, 128), F32),
            pltpu.VMEM((64, 128), F32),
            pltpu.VMEM((128, 128), F32),
            pltpu.VMEM((128, 128), jnp.int32),
            pltpu.VMEM((CHUNKS, 1, CHUNK), jnp.int32),
            pltpu.VMEM((CHUNKS, 1, CHUNK), F32),
            pltpu.VMEM((8, 128), jnp.int32),
            pltpu.VMEM((CHUNKS, LV, CHUNK), F32),
            pltpu.VMEM((WINDOWS, 2 * LV, WIDE), BF16),
            pltpu.VMEM((PAIRS, WIDE, CHUNK), BF16),
            pltpu.VMEM((PAIRS, 1, CHUNK), F32),
            pltpu.VMEM((3, PAIRS, 1, CHUNK), F32),
            pltpu.VMEM((PAIRS, LV, WIDE), F32),
            pltpu.VMEM((VARS, LEVB, ROWS, NX), F32),
            pltpu.SMEM((8, 128), jnp.int32),
            dma((2,)), dma((2,)), dma((3, 2)), dma((3, 2)), dma((3, 2, 3)), dma((3, 2, 3)),
            dma((2,)), dma((2,)), dma((3,)), dma((3,)),
            dma((4, 3, 2)), dma((4, 3, 2)), dma((3,)), dma((3,)), dma((TILES - 1,)), dma((TILES - 1,)),
            dma, dma((VARS,)),
        ],
        compiler_params=pltpu.CompilerParams(
            collective_id=0, has_side_effects=True, vmem_limit_bytes=56 * 1024 * 1024),
    )(
        increment, courant_x, courant_y, level_inverse, profile.transpose(1, 0, 2),
        send_column.reshape(64, 128), send_block.reshape(64, 128), obs_weight.reshape(64, 1, 128),
        coupling, send_count,
    )


def solution(mesh):
    return jax.shard_map(
        shards,
        mesh=mesh,
        in_specs=(
            P("band", None, "tile", None),
            P("band", "tile", None),
            P("band", "tile", None),
            P(None, "band", None),
            P(),
            P("band", None, None),
            P("tile", None),
            P("tile", None),
            P("tile", None),
            P("tile", None),
        ),
        out_specs=P("band", None, "tile", None),
        check_vma=False,
    )
```

```python
import functools

import jax
import jax.numpy as jnp
from jax import lax
from jax.experimental import pallas as pl
from jax.experimental.pallas import tpu as pltpu
from jax.sharding import PartitionSpec as P

MESH = pl.DeviceIdType.MESH
VARS = 5
LEVB = 16
LV = VARS * LEVB
ROWS = 8
NX = 768
BANDS = 4
TILES = 32
CHUNK = 256
CHUNKS = 32
WIDE = 256
WINDOWS = 24
PAIRS = 56
NBLK = 64
INNER_FIRST = (1, 2, 3, 4, 5, 6, 0, 7)
PARTS = ((0, 4), (4, 8), (8, 11), (11, 14))
OUTER_FIRST = (0, 7, 1, 2, 3, 4, 5, 6)
SPLIT = 24
F32 = jnp.float32
BF16 = jnp.bfloat16


def halves(value):
    high = value.astype(BF16)
    low = (value - high.astype(F32)).astype(BF16)
    return high, low


def mm(a, b):
    return jnp.dot(a, b, preferred_element_type=F32)


def wide(value):
    return jnp.concatenate([value] * (NX // 128), axis=1)


def sort_pairs(keys, payload):
    shape = keys.shape
    slab, sub, lane = (lax.broadcasted_iota(jnp.int32, shape, axis) for axis in range(3))
    place = lane * 64 + sub * 8 + slab
    for k in range(1, 14):
        for j in range(k - 1, -1, -1):
            distance = 1 << j
            bit, block = (place >> j) & 1, (place >> k) & 1
            flip = bit != block
            if j < 3:
                def partner(x):
                    parts = x.reshape(8 >> (j + 1), 2, distance, 8, 128)
                    return jnp.concatenate([parts[:, 1:], parts[:, :1]], axis=1).reshape(shape)
            else:
                axis, step, size = (1, distance >> 3, 8) if j < 6 else (2, distance >> 6, 128)

                def partner(x):
                    if 2 * step == size:
                        return pltpu.roll(x, step, axis)
                    return jnp.where(bit == 1, pltpu.roll(x, step, axis), pltpu.roll(x, size - step, axis))
            other, other_payload = partner(keys), partner(payload)
            take = jnp.where(flip, (keys < other).astype(jnp.int32), (keys > other).astype(jnp.int32)) == 1
            keys = jnp.where(take, other, keys)
            payload = jnp.where(take, other_payload, payload)
    return keys, payload


def kernel(
    inc_ref, cx_ref, cy_ref, inv_ref, prof_ref, column_ref, block_ref, weight_ref, coupling_ref, count_ref,
    out_ref,
    field, cyh, co, adj, local, stack, mext, gm, cols, tab, tabl, tabr, edges, recv, beside, corner, coefs, wbuf, wrow, turn, turn_key, keyr, wgtr, pairv,
    ps, xs, onehot, val, valr, acc, finals, pair_ref,
    first_s, first_r, second_s, second_r, halo_s, halo_r, diag_s, diag_r, cy_s, cy_r, cf_s, cf_r, ed_s, ed_r, va_s, va_r, wt_s, wt_r, tab_s, tab_r, pair_sem, out_sem,
):
    band = lax.axis_index("band")
    tile = lax.axis_index("tile")
    north = lax.rem(tile + 1, TILES)
    south = lax.rem(tile + TILES - 1, TILES)
    partner = [lax.rem(band + o, BANDS) for o in (1, 2, 3)]

    barrier = pltpu.get_barrier_semaphore()
    for o in range(1, TILES):
        pl.semaphore_signal(
            barrier, inc=1, device_id={"tile": lax.rem(tile + o, TILES)}, device_id_type=MESH)
    for p in partner:
        pl.semaphore_signal(barrier, inc=1, device_id={"band": p}, device_id_type=MESH)
    for p in partner:
        for t in (north, south):
            pl.semaphore_signal(barrier, inc=1, device_id={"tile": t, "band": p}, device_id_type=MESH)

    sent = []

    def halo(buffer, send, receive):
        up = pltpu.make_async_remote_copy(
            buffer.at[ROWS], buffer.at[0], send.at[0], receive.at[0],
            device_id={"tile": north}, device_id_type=MESH)
        down = pltpu.make_async_remote_copy(
            buffer.at[1], buffer.at[ROWS + 1], send.at[1], receive.at[1],
            device_id={"tile": south}, device_id_type=MESH)
        up.start()
        down.start()
        sent.extend([up, down])
        return up, down

    def band_copy(source, target, send, receive, o):
        copy = pltpu.make_async_remote_copy(
            source, target, send, receive, device_id={"band": partner[o]}, device_id_type=MESH)
        copy.start()
        sent.append(copy)
        return copy

    for v in range(VARS):
        turned = jnp.swapaxes(inc_ref[:, v], 0, 1)
        field[0, 1:ROWS + 1, LEVB * v:LEVB * v + LEVB, :] = turned
    gm[...] = jnp.zeros((2, 128, 128), F32)
    tab[...] = jnp.zeros((LV, 128), F32)
    for v in range(VARS):
        rows = slice(LEVB * v, LEVB * v + LEVB)
        gm[0, rows, rows] = inv_ref[v]
        tab[rows, 0:NBLK] = prof_ref[v]
    gm[1] = gm[0].T
    row_lane = lax.broadcasted_iota(jnp.int32, (8, 128), 1)

    def at_lanes(offset, factors):
        total = jnp.zeros((8, 128), F32)
        for v in range(VARS):
            total = total + jnp.where(row_lane == LEVB * v + offset, factors[v], 0.0)
        return total

    def rows_of(kind, offset):
        rows = [gm[kind, LEVB * v + offset:LEVB * v + offset + 1, :] for v in range(VARS)]
        if kind == 1:
            rows = [coupling_ref[v] * rows[v] for v in range(VARS)]
        return jnp.concatenate(rows + [jnp.zeros((3, 128), F32)], axis=0)

    ones = [1.0] * VARS
    scales = [coupling_ref[v] for v in range(VARS)]
    scale_first, scale_last = at_lanes(0, scales), at_lanes(LEVB - 1, scales)
    one_first, one_last = at_lanes(0, ones), at_lanes(LEVB - 1, ones)
    lasts = [rows_of(kind, LEVB - 1) for kind in range(2)]
    firsts = [rows_of(kind, 0) for kind in range(2)]

    def across(value, weight):
        return jnp.broadcast_to(jnp.sum(value * weight[0:1], axis=1, keepdims=True), (value.shape[0], 128))

    coefs[0, 0] = across(firsts[0], scale_first)
    coefs[0, 1] = across(lasts[0], scale_first)
    coefs[0, 2] = across(firsts[0], scale_last)
    pl.semaphore_wait(barrier, TILES + BANDS - 2 + 2 * (BANDS - 1))
    halo1 = halo(field.at[0], first_s, first_r)
    cf_copies = [
        band_copy(coefs.at[0], coefs.at[o + 1], cf_s.at[o], cf_r.at[o], o) for o in range(3)
    ]
    cols[0, 0] = across(gm[0, :LV], scale_first)
    cols[0, 1] = across(gm[0, :LV], scale_last)
    cols[1, 0] = across(gm[1, :LV], one_first)
    cols[1, 1] = across(gm[1, :LV], one_last)

    wt_copies = []
    for o in range(1, TILES):
        target = lax.rem(tile + o, TILES)
        copy = pltpu.make_async_remote_copy(
            weight_ref.at[pl.ds(2 * target, 2)], wbuf.at[pl.ds(2 * tile, 2)], wt_s.at[o - 1], wt_r.at[o - 1],
            device_id={"tile": target}, device_id_type=MESH)
        copy.start()
        sent.append(copy)
        wt_copies.append(copy)
    cyh[1:ROWS + 1] = jnp.swapaxes(cy_ref[...], 0, 1)
    halo_cy = halo(cyh, cy_s, cy_r)
    co[0] = jnp.swapaxes(cx_ref[...], 0, 1)

    lane = lax.broadcasted_iota(jnp.int32, (LEVB, NX), 1)
    for y in range(ROWS):
        cx = co[0, y]
        cy = cyh[y + 1]
        ax, bx = (jnp.abs(cx) + cx) * 0.5, (jnp.abs(cx) - cx) * 0.5
        ay, by = (jnp.abs(cy) + cy) * 0.5, (jnp.abs(cy) - cy) * 0.5
        co[0, y] = 1.0 - ax - bx - ay - by
        co[1, y] = jnp.where(lane == 0, 0.0, ax)
        co[2, y] = jnp.where(lane == NX - 1, 0.0, bx)
        if y == 0:
            ay = jnp.where(tile == 0, 0.0, ay)
        if y == ROWS - 1:
            by = jnp.where(tile == TILES - 1, 0.0, by)
        co[3, y] = ay
        co[4, y] = by
        adj[0, y] = jnp.where(lane == 0, 0.0, pltpu.roll(bx, 1, 1))
        adj[1, y] = jnp.where(lane == NX - 1, 0.0, pltpu.roll(ax, NX - 1, 1))

    for copy in cf_copies:
        copy.wait_recv()

    def of_band(lane_index):
        result = []
        for j in range(BANDS):
            total = jnp.zeros((8, 128), F32)
            for b in range(BANDS):
                entry = coefs[(b - j) % BANDS, lane_index]
                total = total + jnp.where(band == b, entry, 0.0)
            result.append(total)
        return result

    def select(values):
        total = jnp.zeros((8, 128), F32)
        for b in range(BANDS):
            total = total + jnp.where(band == b, values[b], 0.0)
        return total

    k0, k15, g0 = of_band(0), of_band(1), of_band(2)
    zero = jnp.zeros((8, 128), F32)

    def chain(a, g):
        e = [zero] * (BANDS + 1)
        for j in range(BANDS - 1, -1, -1):
            e[j] = k0[j] + g[j] * e[j + 1] * a[j]
        into_first = select([g[b] * e[b + 1] for b in range(BANDS)])
        own = select([e[b + 1] for b in range(BANDS)])
        low, high = [], []
        for o in (1, 2, 3):
            t_list, s_list = [], []
            for b in range(BANDS):
                j = (b - o) % BANDS
                factor = zero + 1.0
                if j < b:
                    for k in range(j + 1, b):
                        factor = factor * a[k]
                    t_list.append(factor)
                    s_list.append(e[b + 1] * a[b] * factor)
                else:
                    for k in range(b + 1, j):
                        factor = factor * g[k]
                    t_list.append(zero)
                    s_list.append(factor)
            low.append(select(t_list))
            high.append(select(s_list))
        return into_first, own, low, high

    chains = (chain(k15, g0), chain(g0, k15))
    for kind in range(2):
        first = firsts[kind] + chains[kind][0] * lasts[kind]
        matrix = jnp.concatenate([gm[kind, :LV, :], lasts[kind], first], axis=0)[:, :LV]
        high, low = halves(matrix)
        mext[kind] = jnp.concatenate([high, high, low], axis=1)

    high, low = halves(tab[...])
    tabl[...] = mm(mext[1], jnp.concatenate([high, low, high], axis=0)).reshape(12, 8, 128)
    tab_copies = [
        band_copy(tabl.at[10 + (band + o + 1) // BANDS], tabr.at[o], tab_s.at[o], tab_r.at[o], o) for o in range(3)
    ]

    def stencil(src, y, v, kind):
        rows = slice(LEVB * v, LEVB * v + LEVB)
        f = field[src, y + 1, rows, :]
        west, east = pltpu.roll(f, 1, 1), pltpu.roll(f, NX - 1, 1)
        if kind == 0:
            cw, ce, cs, cn = (co[i, y] for i in (1, 2, 3, 4))
        else:
            cw, ce, cs, cn = adj[0, y], adj[1, y], adj[2, y], adj[3, y]
        return (
            co[0, y] * f + cw * west + ce * east
            + cs * field[src, y, rows, :] + cn * field[src, y + 2, rows, :]
        )

    def solve(stage, kind, order, row_value, store_row, before=None, gap=None):
        copies, halos = [], []
        for k, y in enumerate(order):
            if k == 6 and before is not None:
                before()
            for v in range(VARS):
                high, low = halves(row_value(y, v))
                rows = slice(LEVB * v, LEVB * v + LEVB)
                stack[k % 2, rows, :] = high
                stack[k % 2, LV + LEVB * v:LV + LEVB * v + LEVB, :] = low
                stack[k % 2, 2 * LV + LEVB * v:2 * LV + LEVB * v + LEVB, :] = high
            result = mm(mext[kind], stack[k % 2])
            local[stage, y] = result.reshape(12, 8, NX)
            edges[stage, 0, VARS * k:VARS * k + VARS, :] = result[LV:LV + VARS]
            edges[stage, 1, VARS * k:VARS * k + VARS, :] = result[LV + 8:LV + 8 + VARS]
            if y in (0, ROWS - 1):
                side, target = (1, south) if y == 0 else (0, north)
                copy = pltpu.make_async_remote_copy(
                    local.at[stage, y, 0:11], beside.at[stage, side], halo_s.at[stage, side], halo_r.at[stage, side],
                    device_id={"tile": target}, device_id_type=MESH)
                copy.start()
                halos.append(copy)
                for o in range(3):
                    above = (band + o + 1) // BANDS
                    copy = pltpu.make_async_remote_copy(
                        local.at[stage, y, 10 + above], corner.at[stage, side, o],
                        diag_s.at[stage, side, o], diag_r.at[stage, side, o],
                        device_id={"tile": target, "band": partner[o]}, device_id_type=MESH)
                    copy.start()
                    halos.append(copy)
            for part, (at, lo, hi) in enumerate(((4, 0, SPLIT), (7, SPLIT, VARS * ROWS))):
                if k == at:
                    for o in range(3):
                        above = (band + o + 1) // BANDS
                        copies.append(band_copy(
                            edges.at[stage, above, lo:hi], recv.at[stage, o, lo:hi],
                            ed_s.at[stage, o, part], ed_r.at[stage, o, part], o))
        sent.extend(halos)
        if gap is not None:
            gap()
        _, own, low_c, high_c = chains[kind]

        def complete(y, mine, got, parts):
            t = jnp.zeros((VARS, NX), F32)
            s = wide(own[:VARS]) * mine
            for o in range(3):
                t = t + wide(low_c[o][:VARS]) * got[o]
                s = s + wide(high_c[o][:VARS]) * got[o]
            for v in range(VARS):
                rows = slice(LEVB * v, LEVB * v + LEVB)
                left, right = wide(cols[kind, 0, rows, :]), wide(cols[kind, 1, rows, :])
                store_row(y, v, parts(v) + left * t[v:v + 1] + right * s[v:v + 1])

        for copy in copies:
            copy.wait_recv()
        for k, y in enumerate(order):
            span = slice(VARS * k, VARS * k + VARS)
            complete(
                y, edges[stage, 0, span, :], [recv[stage, o, span, :] for o in range(3)],
                lambda v: local[stage, y, 2 * v:2 * v + 2].reshape(LEVB, NX))
        for copy in halos:
            copy.wait_recv()
        for side, y in ((0, -1), (1, ROWS)):
            complete(
                y, beside[stage, side, 10][:VARS], [corner[stage, side, o][:VARS] for o in range(3)],
                lambda v: beside[stage, side, 2 * v:2 * v + 2].reshape(LEVB, NX))

    def wait_halo(copies):
        for copy in copies:
            copy.wait_recv()

    def into_field(index):
        def store(y, v, value):
            field[index, y + 1, LEVB * v:LEVB * v + LEVB, :] = value
        return store

    def store_state(y, v, value):
        high, low = halves(value)
        for j in range(3):
            cols = slice(WIDE * j, WIDE * j + WIDE)
            xs[3 * y + j, LEVB * v:LEVB * v + LEVB, :] = high[:, cols]
            xs[3 * y + j, LV + LEVB * v:LV + LEVB * v + LEVB, :] = low[:, cols]

    def sort_slots():
        for copy in wt_copies:
            copy.wait_recv()
        own = pl.ds(2 * tile, 2)
        wbuf[own] = weight_ref[own]
        slot = lax.broadcasted_iota(jnp.int32, (1, 128), 1)
        for r in range(64):
            live = slot < count_ref[0, r // 2] - 128 * (r % 2)
            wrow[r:r + 1, :] = jnp.where(live, wbuf[r], 0.0)
        keys = (column_ref[...] * NBLK + block_ref[...]).reshape(8, 8, 128)
        keys, weights = sort_pairs(keys, wrow[...].reshape(8, 8, 128))
        turn_key[0:64, :] = keys.reshape(64, 128)
        turn_key[64:128, :] = jnp.zeros((64, 128), jnp.int32)
        turn_key[...] = turn_key[...].T
        turn[0:64, :] = weights.reshape(64, 128)
        turn[64:128, :] = jnp.zeros((64, 128), F32)
        turn[...] = turn[...].T

        def rows_of_chunks(ref):
            return jnp.concatenate(
                [ref[pl.ds(q, CHUNKS, stride=4), :][:, :64] for q in range(4)], axis=1)

        rows, weights = rows_of_chunks(turn_key), rows_of_chunks(turn)
        for c in range(CHUNKS):
            keyr[c] = rows[c:c + 1]
            wgtr[c] = weights[c:c + 1]
        first = jnp.broadcast_to(rows[:, 0:1] // (NBLK * WIDE), (CHUNKS, 128))
        last = jnp.broadcast_to(rows[:, CHUNK - 1:CHUNK] // (NBLK * WIDE), (CHUNKS, 128))
        number = last - first + 1
        sub = lax.broadcasted_iota(jnp.int32, (CHUNKS, 128), 0)
        p = lax.broadcasted_iota(jnp.int32, (CHUNKS, 128), 1)
        upto = number
        for d in (1, 2, 4, 8, 16):
            upto = upto + jnp.where(sub >= d, pltpu.roll(upto, d, 0), 0)
        start = upto - number

        def down(value):
            return jnp.sum(value, axis=0, keepdims=True)

        chunk = jnp.clip(down(jnp.where(start <= p, 1, 0)) - 1, 0, CHUNKS - 1)
        window = down(jnp.where(sub == chunk, first - start + p, 0))
        valid = p[0:1] < upto[CHUNKS - 1:CHUNKS]
        index = jnp.clip(jnp.where(valid, window, WINDOWS - 1), 0, WINDOWS - 1)
        base = jnp.where(valid, window * WIDE, -(1 << 20))
        same = jnp.where((p[0:1] > 0) & (index == pltpu.roll(index, 1, 1)), 1, 0)
        latest = jnp.clip(down(jnp.clip(p - first + 1, 0, number)) - 1, 0, PAIRS - 1)
        some = jnp.minimum(down(jnp.where((first <= p) & (p <= last), 1, 0)), 1)
        zeros = jnp.zeros((2, 128), jnp.int32)
        pairv[...] = jnp.concatenate([chunk, index, base, same, latest, some, zeros], axis=0)
        copy = pltpu.make_async_copy(pairv, pair_ref, pair_sem)
        copy.start()
        copy.wait()

    def pick_slots():
        for copy in tab_copies:
            copy.wait_recv()
        _, own, low_c, high_c = chains[1]
        t = jnp.zeros((8, 128), F32)
        s = own * tabl[10]
        for o in range(3):
            t = t + low_c[o] * tabr[o]
            s = s + high_c[o] * tabr[o]
        for v in range(VARS):
            rows = slice(LEVB * v, LEVB * v + LEVB)
            tab[rows, :] = (
                tabl[2 * v:2 * v + 2].reshape(LEVB, 128)
                + cols[1, 0, rows, :] * t[v:v + 1] + cols[1, 1, rows, :] * s[v:v + 1])
        profiles = jnp.concatenate(halves(tab[:, 0:NBLK]), axis=0)
        block_iota = lax.broadcasted_iota(jnp.int32, (NBLK, CHUNK), 0)
        cell_iota = lax.broadcasted_iota(jnp.int32, (WIDE, CHUNK), 0)

        def pick_profiles(i, carry):
            for u in range(4):
                c = 4 * i + u
                picked = mm(profiles, (block_iota == keyr[c] % NBLK).astype(BF16))
                ps[c] = picked[:LV] + picked[LV:]
            return carry

        lax.fori_loop(0, CHUNKS // 4, pick_profiles, 0)

        def pick_cells(i, carry):
            for u in range(4):
                p = 4 * i + u
                onehot[p] = (cell_iota == keyr[pair_ref[0, p]] // NBLK - pair_ref[2, p]).astype(BF16)
            return carry

        lax.fori_loop(0, PAIRS // 4, pick_cells, 0)

    def gap():
        sort_slots()
        pick_slots()

    solve(
        0, 0, INNER_FIRST, lambda y, v: stencil(0, y, v, 0), into_field(1),
        before=lambda: wait_halo(halo1), gap=gap)
    for y in range(ROWS):
        for v in range(VARS):
            store_state(y, v, stencil(1, y, v, 0))

    def observe(i, carry):
        for u in range(4):
            p = 4 * i + u
            picked = mm(xs[pair_ref[1, p]], onehot[p])
            product = (picked[:LV] + picked[LV:]) * ps[pair_ref[0, p]]
            val[p] = jnp.sum(product, axis=0, keepdims=True)
        return carry

    copies = []
    for n, (begin, end) in enumerate(PARTS):
        lax.fori_loop(begin, end, observe, 0)
        span = slice(4 * begin, 4 * end)
        copies.append([
            band_copy(val.at[span], valr.at[o, span], va_s.at[n, o], va_r.at[n, o], o) for o in range(3)])

    wait_halo(halo_cy)
    for y in range(ROWS):
        below, above = cyh[y], cyh[y + 2]
        by = (jnp.abs(below) - below) * 0.5
        ay = (jnp.abs(above) + above) * 0.5
        if y == 0:
            by = jnp.where(tile == 0, 0.0, by)
        if y == ROWS - 1:
            ay = jnp.where(tile == TILES - 1, 0.0, ay)
        adj[2, y] = by
        adj[3, y] = ay
    def spread(i, before):
        for u in range(4):
            p = 4 * i + u
            c = pair_ref[0, p]
            values = (val[p] + valr[0, p]) + (valr[1, p] + valr[2, p])
            high, low = halves(ps[c] * (values * wgtr[c]))
            both = jnp.concatenate([high, low], axis=0)
            added = lax.dot_general(
                both, onehot[p], (((1,), (1,)), ((), ())), preferred_element_type=F32)
            before = before * pair_ref[3, p].astype(F32) + (added[:LV] + added[LV:])
            acc[p] = before
        return before

    total = jnp.zeros((LV, WIDE), F32)
    for part, (begin, end) in zip(copies, PARTS):
        wait_halo(part)
        total = lax.fori_loop(begin, end, spread, total)

    for y in OUTER_FIRST:
        for j in range(3):
            w = 3 * y + j
            field[2, y + 1, :, WIDE * j:WIDE * j + WIDE] = acc[pair_ref[4, w]] * pair_ref[5, w].astype(F32)
        if y == ROWS - 1:
            halo2 = halo(field.at[2], second_s, second_r)
    solve(
        1, 1, INNER_FIRST, lambda y, v: stencil(2, y, v, 1), into_field(3),
        before=lambda: wait_halo(halo2))

    outs = []
    for v in range(VARS):
        rows = slice(LEVB * v, LEVB * v + LEVB)
        result = [stencil(3, y, v, 1) + field[0, y + 1, rows, :] for y in range(ROWS)]
        out_stage = finals.at[v]
        out_stage[...] = jnp.swapaxes(jnp.stack(result), 0, 1)
        outs.append(pltpu.make_async_copy(out_stage, out_ref.at[:, v], out_sem.at[v]))
        outs[-1].start()
    for copy in outs:
        copy.wait()
    for copy in sent:
        copy.wait_send()


def shards(
    increment, courant_x, courant_y, level_inverse, coupling, profile, send_column, send_block, send_count, obs_weight,
):
    vmem = pl.BlockSpec(memory_space=pltpu.VMEM)
    smem = pl.BlockSpec(memory_space=pltpu.SMEM)
    dma = pltpu.SemaphoreType.DMA
    return pl.pallas_call(
        kernel,
        out_shape=jax.ShapeDtypeStruct(increment.shape, F32),
        in_specs=[vmem] * 8 + [smem] * 2,
        out_specs=pl.BlockSpec(memory_space=pl.ANY),
        scratch_shapes=[
            pltpu.VMEM((4, ROWS + 2, LV, NX), F32),
            pltpu.VMEM((ROWS + 2, LEVB, NX), F32),
            pltpu.VMEM((5, ROWS, LEVB, NX), F32),
            pltpu.VMEM((4, ROWS, LEVB, NX), F32),
            pltpu.VMEM((2, ROWS, 12, 8, NX), F32),
            pltpu.VMEM((2, 3 * LV, NX), BF16),
            pltpu.VMEM((2, LV + 16, 3 * LV), BF16),
            pltpu.VMEM((2, 128, 128), F32),
            pltpu.VMEM((2, 2, LV, 128), F32),
            pltpu.VMEM((LV, 128), F32),
            pltpu.VMEM((12, 8, 128), F32),
            pltpu.VMEM((3, 8, 128), F32),
            pltpu.VMEM((2, 2, VARS * ROWS, NX), F32),
            pltpu.VMEM((2, 3, VARS * ROWS, NX), F32),
            pltpu.VMEM((2, 2, 11, 8, NX), F32),
            pltpu.VMEM((2, 2, 3, 8, NX), F32),
            pltpu.VMEM((4, 3, 8, 128), F32),
            pltpu.VMEM((64, 1, 128), F32),
            pltpu.VMEM((64, 128), F32),
            pltpu.VMEM((128, 128), F32),
            pltpu.VMEM((128, 128), jnp.int32),
            pltpu.VMEM((CHUNKS, 1, CHUNK), jnp.int32),
            pltpu.VMEM((CHUNKS, 1, CHUNK), F32),
            pltpu.VMEM((8, 128), jnp.int32),
            pltpu.VMEM((CHUNKS, LV, CHUNK), F32),
            pltpu.VMEM((WINDOWS, 2 * LV, WIDE), BF16),
            pltpu.VMEM((PAIRS, WIDE, CHUNK), BF16),
            pltpu.VMEM((PAIRS, 1, CHUNK), F32),
            pltpu.VMEM((3, PAIRS, 1, CHUNK), F32),
            pltpu.VMEM((PAIRS, LV, WIDE), F32),
            pltpu.VMEM((VARS, LEVB, ROWS, NX), F32),
            pltpu.SMEM((8, 128), jnp.int32),
            dma((2,)), dma((2,)), dma((2,)), dma((2,)), dma((2, 2)), dma((2, 2)), dma((2, 2, 3)), dma((2, 2, 3)),
            dma((2,)), dma((2,)), dma((3,)), dma((3,)),
            dma((2, 3, 2)), dma((2, 3, 2)), dma((4, 3)), dma((4, 3)), dma((TILES - 1,)), dma((TILES - 1,)),
            dma((3,)), dma((3,)),
            dma, dma((VARS,)),
        ],
        compiler_params=pltpu.CompilerParams(
            collective_id=0, has_side_effects=True, vmem_limit_bytes=56 * 1024 * 1024),
    )(
        increment, courant_x, courant_y, level_inverse, profile.transpose(1, 0, 2),
        send_column.reshape(64, 128), send_block.reshape(64, 128), obs_weight.reshape(64, 1, 128),
        coupling, send_count,
    )


def solution(mesh):
    return jax.shard_map(
        shards,
        mesh=mesh,
        in_specs=(
            P("band", None, "tile", None),
            P("band", "tile", None),
            P("band", "tile", None),
            P(None, "band", None),
            P(),
            P("band", None, None),
            P("tile", None),
            P("tile", None),
            P("tile", None),
            P("tile", None),
        ),
        out_specs=P("band", None, "tile", None),
        check_vma=False,
    )
```

```python
import functools

import jax
import jax.numpy as jnp
from jax import lax
from jax.experimental import pallas as pl
from jax.experimental.pallas import tpu as pltpu
from jax.sharding import PartitionSpec as P

MESH = pl.DeviceIdType.MESH
VARS = 5
LEVB = 16
LV = VARS * LEVB
ROWS = 8
NX = 768
BANDS = 4
TILES = 32
CHUNK = 256
CHUNKS = 32
WIDE = 256
WINDOWS = 24
PAIRS = 56
NBLK = 64
INNER_FIRST = (1, 2, 3, 4, 5, 6, 0, 7)
PARTS = ((0, 4), (4, 8), (8, 11), (11, 14))
SPLIT = 24
F32 = jnp.float32
BF16 = jnp.bfloat16


def halves(value):
    high = value.astype(BF16)
    low = (value - high.astype(F32)).astype(BF16)
    return high, low


def mm(a, b):
    return jnp.dot(a, b, preferred_element_type=F32)


def wide(value):
    return jnp.concatenate([value] * (NX // 128), axis=1)


def sort_pairs(keys, payload):
    shape = keys.shape
    slab, sub, lane = (lax.broadcasted_iota(jnp.int32, shape, axis) for axis in range(3))
    place = lane * 64 + sub * 8 + slab
    for k in range(1, 14):
        for j in range(k - 1, -1, -1):
            distance = 1 << j
            bit, block = (place >> j) & 1, (place >> k) & 1
            flip = bit != block
            if j < 3:
                def partner(x):
                    parts = x.reshape(8 >> (j + 1), 2, distance, 8, 128)
                    return jnp.concatenate([parts[:, 1:], parts[:, :1]], axis=1).reshape(shape)
            else:
                axis, step, size = (1, distance >> 3, 8) if j < 6 else (2, distance >> 6, 128)

                def partner(x):
                    if 2 * step == size:
                        return pltpu.roll(x, step, axis)
                    return jnp.where(bit == 1, pltpu.roll(x, step, axis), pltpu.roll(x, size - step, axis))
            other, other_payload = partner(keys), partner(payload)
            take = jnp.where(flip, (keys < other).astype(jnp.int32), (keys > other).astype(jnp.int32)) == 1
            keys = jnp.where(take, other, keys)
            payload = jnp.where(take, other_payload, payload)
    return keys, payload


def kernel(
    inc_hbm, cx_hbm, cy_hbm, inv_ref, prof_ref, column_ref, block_ref, weight_ref, coupling_ref, count_ref,
    out_ref,
    field, cyh, co, adj, partial, local, stack, mext, gm, cols, tab, tabl, tabr, edges, recv, beside, corner, coefs, wbuf, wrow, turn, turn_key, keyr, wgtr, pairv,
    ps, xs, onehot, val, valr, acc, inc_ref, cx_ref, cy_ref, pair_ref,
    first_s, first_r, second_s, second_r, halo_s, halo_r, diag_s, diag_r, cy_s, cy_r, cf_s, cf_r, ed_s, ed_r, va_s, va_r, wt_s, wt_r, tab_s, tab_r, pair_sem, out_sem, in_sem,
):
    band = lax.axis_index("band")
    tile = lax.axis_index("tile")
    north = lax.rem(tile + 1, TILES)
    south = lax.rem(tile + TILES - 1, TILES)
    partner = [lax.rem(band + o, BANDS) for o in (1, 2, 3)]

    barrier = pltpu.get_barrier_semaphore()
    for o in range(1, TILES):
        pl.semaphore_signal(
            barrier, inc=1, device_id={"tile": lax.rem(tile + o, TILES)}, device_id_type=MESH)
    for p in partner:
        pl.semaphore_signal(barrier, inc=1, device_id={"band": p}, device_id_type=MESH)
    for p in partner:
        for t in (north, south):
            pl.semaphore_signal(barrier, inc=1, device_id={"tile": t, "band": p}, device_id_type=MESH)

    sent = []

    def halo(buffer, send, receive):
        up = pltpu.make_async_remote_copy(
            buffer.at[ROWS], buffer.at[0], send.at[0], receive.at[0],
            device_id={"tile": north}, device_id_type=MESH)
        down = pltpu.make_async_remote_copy(
            buffer.at[1], buffer.at[ROWS + 1], send.at[1], receive.at[1],
            device_id={"tile": south}, device_id_type=MESH)
        up.start()
        down.start()
        sent.extend([up, down])
        return up, down

    def halo_part(buffer, c, send, receive):
        cols = slice(WIDE * c, WIDE * c + WIDE)
        pair = []
        for n, (source, target, place) in enumerate(((ROWS, north, 0), (1, south, ROWS + 1))):
            copy = pltpu.make_async_remote_copy(
                buffer.at[source, :, cols], buffer.at[place, :, cols], send.at[n, c], receive.at[n, c],
                device_id={"tile": target}, device_id_type=MESH)
            copy.start()
            pair.append(copy)
        sent.extend(pair)
        return pair

    def band_copy(source, target, send, receive, o):
        copy = pltpu.make_async_remote_copy(
            source, target, send, receive, device_id={"band": partner[o]}, device_id_type=MESH)
        copy.start()
        sent.append(copy)
        return copy

    loads = [pltpu.make_async_copy(inc_hbm.at[:, v], inc_ref.at[v], in_sem.at[v]) for v in range(VARS)]
    loads.append(pltpu.make_async_copy(cy_hbm, cy_ref, in_sem.at[VARS]))
    loads.append(pltpu.make_async_copy(cx_hbm, cx_ref, in_sem.at[VARS + 1]))
    for copy in loads:
        copy.start()

    gm[...] = jnp.zeros((2, 128, 128), F32)
    tab[...] = jnp.zeros((LV, 128), F32)
    for v in range(VARS):
        rows = slice(LEVB * v, LEVB * v + LEVB)
        gm[0, rows, rows] = inv_ref[v]
        tab[rows, 0:NBLK] = prof_ref[v]
    gm[1] = gm[0].T
    row_lane = lax.broadcasted_iota(jnp.int32, (8, 128), 1)

    def at_lanes(offset, factors):
        total = jnp.zeros((8, 128), F32)
        for v in range(VARS):
            total = total + jnp.where(row_lane == LEVB * v + offset, factors[v], 0.0)
        return total

    def rows_of(kind, offset):
        rows = [gm[kind, LEVB * v + offset:LEVB * v + offset + 1, :] for v in range(VARS)]
        if kind == 1:
            rows = [coupling_ref[v] * rows[v] for v in range(VARS)]
        return jnp.concatenate(rows + [jnp.zeros((3, 128), F32)], axis=0)

    ones = [1.0] * VARS
    scales = [coupling_ref[v] for v in range(VARS)]
    scale_first, scale_last = at_lanes(0, scales), at_lanes(LEVB - 1, scales)
    one_first, one_last = at_lanes(0, ones), at_lanes(LEVB - 1, ones)
    lasts = [rows_of(kind, LEVB - 1) for kind in range(2)]
    firsts = [rows_of(kind, 0) for kind in range(2)]

    def across(value, weight):
        return jnp.broadcast_to(jnp.sum(value * weight[0:1], axis=1, keepdims=True), (value.shape[0], 128))

    for v in range(VARS):
        loads[v].wait()
        turned = jnp.swapaxes(inc_ref[v], 0, 1)
        field[0, 1:ROWS + 1, LEVB * v:LEVB * v + LEVB, :] = turned
    coefs[0, 0] = across(firsts[0], scale_first)
    coefs[0, 1] = across(lasts[0], scale_first)
    coefs[0, 2] = across(firsts[0], scale_last)
    pl.semaphore_wait(barrier, TILES + BANDS - 2 + 2 * (BANDS - 1))
    halo1 = [halo_part(field.at[0], c, first_s, first_r) for c in range(3)]
    cf_copies = [
        band_copy(coefs.at[0], coefs.at[o + 1], cf_s.at[o], cf_r.at[o], o) for o in range(3)
    ]
    cols[0, 0] = across(gm[0, :LV], scale_first)
    cols[0, 1] = across(gm[0, :LV], scale_last)
    cols[1, 0] = across(gm[1, :LV], one_first)
    cols[1, 1] = across(gm[1, :LV], one_last)

    wt_copies = []
    for o in range(1, TILES):
        target = lax.rem(tile + o, TILES)
        copy = pltpu.make_async_remote_copy(
            weight_ref.at[pl.ds(2 * target, 2)], wbuf.at[pl.ds(2 * tile, 2)], wt_s.at[o - 1], wt_r.at[o - 1],
            device_id={"tile": target}, device_id_type=MESH)
        copy.start()
        sent.append(copy)
        wt_copies.append(copy)
    loads[VARS].wait()
    loads[VARS + 1].wait()
    cyh[1:ROWS + 1] = jnp.swapaxes(cy_ref[...], 0, 1)
    halo_cy = halo(cyh, cy_s, cy_r)
    co[0] = jnp.swapaxes(cx_ref[...], 0, 1)

    lane = lax.broadcasted_iota(jnp.int32, (LEVB, NX), 1)
    for y in range(ROWS):
        cx = co[0, y]
        cy = cyh[y + 1]
        ax, bx = (jnp.abs(cx) + cx) * 0.5, (jnp.abs(cx) - cx) * 0.5
        ay, by = (jnp.abs(cy) + cy) * 0.5, (jnp.abs(cy) - cy) * 0.5
        co[0, y] = 1.0 - ax - bx - ay - by
        co[1, y] = jnp.where(lane == 0, 0.0, ax)
        co[2, y] = jnp.where(lane == NX - 1, 0.0, bx)
        if y == 0:
            ay = jnp.where(tile == 0, 0.0, ay)
        if y == ROWS - 1:
            by = jnp.where(tile == TILES - 1, 0.0, by)
        co[3, y] = ay
        co[4, y] = by
        adj[0, y] = jnp.where(lane == 0, 0.0, pltpu.roll(bx, 1, 1))
        adj[1, y] = jnp.where(lane == NX - 1, 0.0, pltpu.roll(ax, NX - 1, 1))

    for copy in cf_copies:
        copy.wait_recv()

    def of_band(lane_index):
        result = []
        for j in range(BANDS):
            total = jnp.zeros((8, 128), F32)
            for b in range(BANDS):
                entry = coefs[(b - j) % BANDS, lane_index]
                total = total + jnp.where(band == b, entry, 0.0)
            result.append(total)
        return result

    def select(values):
        total = jnp.zeros((8, 128), F32)
        for b in range(BANDS):
            total = total + jnp.where(band == b, values[b], 0.0)
        return total

    k0, k15, g0 = of_band(0), of_band(1), of_band(2)
    zero = jnp.zeros((8, 128), F32)

    def chain(a, g):
        e = [zero] * (BANDS + 1)
        for j in range(BANDS - 1, -1, -1):
            e[j] = k0[j] + g[j] * e[j + 1] * a[j]
        into_first = select([g[b] * e[b + 1] for b in range(BANDS)])
        own = select([e[b + 1] for b in range(BANDS)])
        low, high = [], []
        for o in (1, 2, 3):
            t_list, s_list = [], []
            for b in range(BANDS):
                j = (b - o) % BANDS
                factor = zero + 1.0
                if j < b:
                    for k in range(j + 1, b):
                        factor = factor * a[k]
                    t_list.append(factor)
                    s_list.append(e[b + 1] * a[b] * factor)
                else:
                    for k in range(b + 1, j):
                        factor = factor * g[k]
                    t_list.append(zero)
                    s_list.append(factor)
            low.append(select(t_list))
            high.append(select(s_list))
        return into_first, own, low, high

    chains = (chain(k15, g0), chain(g0, k15))
    for kind in range(2):
        first = firsts[kind] + chains[kind][0] * lasts[kind]
        matrix = jnp.concatenate([gm[kind, :LV, :], lasts[kind], first], axis=0)[:, :LV]
        high, low = halves(matrix)
        mext[kind] = jnp.concatenate([high, high, low], axis=1)

    high, low = halves(tab[...])
    tabl[...] = mm(mext[1], jnp.concatenate([high, low, high], axis=0)).reshape(12, 8, 128)
    tab_copies = [
        band_copy(tabl.at[10 + (band + o + 1) // BANDS], tabr.at[o], tab_s.at[o], tab_r.at[o], o) for o in range(3)
    ]

    def stencil(src, y, v, kind, below=True, above=True):
        rows = slice(LEVB * v, LEVB * v + LEVB)
        f = field[src, y + 1, rows, :]
        west, east = pltpu.roll(f, 1, 1), pltpu.roll(f, NX - 1, 1)
        cw, ce = (co[1, y], co[2, y]) if kind == 0 else (adj[0, y], adj[1, y])
        result = co[0, y] * f + cw * west + ce * east
        if below:
            result = result + (co[3, y] if kind == 0 else adj[2, y]) * field[src, y, rows, :]
        if above:
            result = result + (co[4, y] if kind == 0 else adj[3, y]) * field[src, y + 2, rows, :]
        return result

    def solve(stage, kind, src, arrivals, store_row, gap=None):
        copies, halos = [], []
        order = INNER_FIRST

        def multiply(y, k, slot, part_cols, value):
            for v in range(VARS):
                high, low = halves(value(v))
                for n, half in enumerate((high, low, high)):
                    stack[slot, LV * n + LEVB * v:LV * n + LEVB * v + LEVB, part_cols] = half
            result = mm(mext[kind], stack[slot, :, part_cols])
            local[stage, y, :, :, part_cols] = result.reshape(12, 8, result.shape[1])
            edges[stage, 0, VARS * k:VARS * k + VARS, part_cols] = result[LV:LV + VARS]
            edges[stage, 1, VARS * k:VARS * k + VARS, part_cols] = result[LV + 8:LV + 8 + VARS]

        def send_edges(part, lo, hi):
            for o in range(3):
                above = (band + o + 1) // BANDS
                copies.append(band_copy(
                    edges.at[stage, above, lo:hi], recv.at[stage, o, lo:hi],
                    ed_s.at[stage, o, part], ed_r.at[stage, o, part], o))

        for k, y in enumerate(order[:6]):
            multiply(y, k, k % 2, slice(0, NX), lambda v: stencil(src, y, v, kind))
            if k == 4:
                send_edges(0, 0, SPLIT)
        outer = ((0, 0, 1, south), (ROWS - 1, ROWS + 1, 0, north))
        for i, (y, beyond, side, target) in enumerate(outer):
            for v in range(VARS):
                partial[i, LEVB * v:LEVB * v + LEVB, :] = stencil(src, y, v, kind, y > 0, y == 0)
        for c in range(3):
            part_cols = slice(WIDE * c, WIDE * c + WIDE)
            wait_halo(arrivals[c])
            for i, (y, beyond, side, target) in enumerate(outer):
                factor = (co[3 + i, y, :, part_cols]) if kind == 0 else adj[2 + i, y, :, part_cols]

                def value(v):
                    rows = slice(LEVB * v, LEVB * v + LEVB)
                    return partial[i, rows, part_cols] + factor * field[src, beyond, rows, part_cols]

                multiply(y, 6 + i, i, part_cols, value)
                copy = pltpu.make_async_remote_copy(
                    local.at[stage, y, 0:11, :, part_cols], beside.at[stage, side, :, :, part_cols],
                    halo_s.at[stage, side, c], halo_r.at[stage, side, c],
                    device_id={"tile": target}, device_id_type=MESH)
                copy.start()
                halos.append(copy)
        send_edges(1, SPLIT, VARS * ROWS)
        for y, beyond, side, target in outer:
            for o in range(3):
                above = (band + o + 1) // BANDS
                copy = pltpu.make_async_remote_copy(
                    local.at[stage, y, 10 + above], corner.at[stage, side, o],
                    diag_s.at[stage, side, o], diag_r.at[stage, side, o],
                    device_id={"tile": target, "band": partner[o]}, device_id_type=MESH)
                copy.start()
                halos.append(copy)
        sent.extend(halos)
        if gap is not None:
            gap()
        _, own, low_c, high_c = chains[kind]

        def complete(y, mine, got, parts):
            t = jnp.zeros((VARS, NX), F32)
            s = wide(own[:VARS]) * mine
            for o in range(3):
                t = t + wide(low_c[o][:VARS]) * got[o]
                s = s + wide(high_c[o][:VARS]) * got[o]
            for v in range(VARS):
                rows = slice(LEVB * v, LEVB * v + LEVB)
                left, right = wide(cols[kind, 0, rows, :]), wide(cols[kind, 1, rows, :])
                store_row(y, v, parts(v) + left * t[v:v + 1] + right * s[v:v + 1])

        for copy in copies:
            copy.wait_recv()
        for k, y in enumerate(order):
            span = slice(VARS * k, VARS * k + VARS)
            complete(
                y, edges[stage, 0, span, :], [recv[stage, o, span, :] for o in range(3)],
                lambda v: local[stage, y, 2 * v:2 * v + 2].reshape(LEVB, NX))
        for copy in halos:
            copy.wait_recv()
        for side, y in ((0, -1), (1, ROWS)):
            complete(
                y, beside[stage, side, 10][:VARS], [corner[stage, side, o][:VARS] for o in range(3)],
                lambda v: beside[stage, side, 2 * v:2 * v + 2].reshape(LEVB, NX))

    def wait_halo(copies):
        for copy in copies:
            copy.wait_recv()

    def into_field(index):
        def store(y, v, value):
            field[index, y + 1, LEVB * v:LEVB * v + LEVB, :] = value
        return store

    def store_state(y, v, value):
        high, low = halves(value)
        for j in range(3):
            cols = slice(WIDE * j, WIDE * j + WIDE)
            xs[3 * y + j, LEVB * v:LEVB * v + LEVB, :] = high[:, cols]
            xs[3 * y + j, LV + LEVB * v:LV + LEVB * v + LEVB, :] = low[:, cols]

    def sort_slots():
        for copy in wt_copies:
            copy.wait_recv()
        own = pl.ds(2 * tile, 2)
        wbuf[own] = weight_ref[own]
        slot = lax.broadcasted_iota(jnp.int32, (1, 128), 1)
        for r in range(64):
            live = slot < count_ref[0, r // 2] - 128 * (r % 2)
            wrow[r:r + 1, :] = jnp.where(live, wbuf[r], 0.0)
        keys = (column_ref[...] * NBLK + block_ref[...]).reshape(8, 8, 128)
        keys, weights = sort_pairs(keys, wrow[...].reshape(8, 8, 128))
        turn_key[0:64, :] = keys.reshape(64, 128)
        turn_key[64:128, :] = jnp.zeros((64, 128), jnp.int32)
        turn_key[...] = turn_key[...].T
        turn[0:64, :] = weights.reshape(64, 128)
        turn[64:128, :] = jnp.zeros((64, 128), F32)
        turn[...] = turn[...].T

        def rows_of_chunks(ref):
            return jnp.concatenate(
                [ref[pl.ds(q, CHUNKS, stride=4), :][:, :64] for q in range(4)], axis=1)

        rows, weights = rows_of_chunks(turn_key), rows_of_chunks(turn)
        for c in range(CHUNKS):
            keyr[c] = rows[c:c + 1]
            wgtr[c] = weights[c:c + 1]
        first = jnp.broadcast_to(rows[:, 0:1] // (NBLK * WIDE), (CHUNKS, 128))
        last = jnp.broadcast_to(rows[:, CHUNK - 1:CHUNK] // (NBLK * WIDE), (CHUNKS, 128))
        number = last - first + 1
        sub = lax.broadcasted_iota(jnp.int32, (CHUNKS, 128), 0)
        p = lax.broadcasted_iota(jnp.int32, (CHUNKS, 128), 1)
        upto = number
        for d in (1, 2, 4, 8, 16):
            upto = upto + jnp.where(sub >= d, pltpu.roll(upto, d, 0), 0)
        start = upto - number

        def down(value):
            return jnp.sum(value, axis=0, keepdims=True)

        chunk = jnp.clip(down(jnp.where(start <= p, 1, 0)) - 1, 0, CHUNKS - 1)
        window = down(jnp.where(sub == chunk, first - start + p, 0))
        valid = p[0:1] < upto[CHUNKS - 1:CHUNKS]
        index = jnp.clip(jnp.where(valid, window, WINDOWS - 1), 0, WINDOWS - 1)
        base = jnp.where(valid, window * WIDE, -(1 << 20))
        same = jnp.where((p[0:1] > 0) & (index == pltpu.roll(index, 1, 1)), 1, 0)
        latest = jnp.clip(down(jnp.clip(p - first + 1, 0, number)) - 1, 0, PAIRS - 1)
        some = jnp.minimum(down(jnp.where((first <= p) & (p <= last), 1, 0)), 1)
        zeros = jnp.zeros((2, 128), jnp.int32)
        pairv[...] = jnp.concatenate([chunk, index, base, same, latest, some, zeros], axis=0)
        copy = pltpu.make_async_copy(pairv, pair_ref, pair_sem)
        copy.start()
        copy.wait()

    def pick_slots():
        for copy in tab_copies:
            copy.wait_recv()
        _, own, low_c, high_c = chains[1]
        t = jnp.zeros((8, 128), F32)
        s = own * tabl[10]
        for o in range(3):
            t = t + low_c[o] * tabr[o]
            s = s + high_c[o] * tabr[o]
        for v in range(VARS):
            rows = slice(LEVB * v, LEVB * v + LEVB)
            tab[rows, :] = (
                tabl[2 * v:2 * v + 2].reshape(LEVB, 128)
                + cols[1, 0, rows, :] * t[v:v + 1] + cols[1, 1, rows, :] * s[v:v + 1])
        profiles = jnp.concatenate(halves(tab[:, 0:NBLK]), axis=0)
        block_iota = lax.broadcasted_iota(jnp.int32, (NBLK, CHUNK), 0)
        cell_iota = lax.broadcasted_iota(jnp.int32, (WIDE, CHUNK), 0)

        def pick_profiles(i, carry):
            for u in range(4):
                c = 4 * i + u
                picked = mm(profiles, (block_iota == keyr[c] % NBLK).astype(BF16))
                ps[c] = picked[:LV] + picked[LV:]
            return carry

        lax.fori_loop(0, CHUNKS // 4, pick_profiles, 0)

        def pick_cells(i, carry):
            for u in range(4):
                p = 4 * i + u
                onehot[p] = (cell_iota == keyr[pair_ref[0, p]] // NBLK - pair_ref[2, p]).astype(BF16)
            return carry

        lax.fori_loop(0, PAIRS // 4, pick_cells, 0)

    def gap():
        sort_slots()
        pick_slots()

    solve(0, 0, 0, halo1, into_field(1), gap)
    for y in range(ROWS):
        for v in range(VARS):
            store_state(y, v, stencil(1, y, v, 0))

    def observe(i, carry):
        for u in range(4):
            p = 4 * i + u
            picked = mm(xs[pair_ref[1, p]], onehot[p])
            product = (picked[:LV] + picked[LV:]) * ps[pair_ref[0, p]]
            val[p] = jnp.sum(product, axis=0, keepdims=True)
        return carry

    copies = []
    for n, (begin, end) in enumerate(PARTS):
        lax.fori_loop(begin, end, observe, 0)
        span = slice(4 * begin, 4 * end)
        copies.append([
            band_copy(val.at[span], valr.at[o, span], va_s.at[n, o], va_r.at[n, o], o) for o in range(3)])

    wait_halo(halo_cy)
    for y in range(ROWS):
        below, above = cyh[y], cyh[y + 2]
        by = (jnp.abs(below) - below) * 0.5
        ay = (jnp.abs(above) + above) * 0.5
        if y == 0:
            by = jnp.where(tile == 0, 0.0, by)
        if y == ROWS - 1:
            ay = jnp.where(tile == TILES - 1, 0.0, ay)
        adj[2, y] = by
        adj[3, y] = ay
    def spread(i, before):
        for u in range(4):
            p = 4 * i + u
            c = pair_ref[0, p]
            values = (val[p] + valr[0, p]) + (valr[1, p] + valr[2, p])
            high, low = halves(ps[c] * (values * wgtr[c]))
            both = jnp.concatenate([high, low], axis=0)
            added = lax.dot_general(
                both, onehot[p], (((1,), (1,)), ((), ())), preferred_element_type=F32)
            before = before * pair_ref[3, p].astype(F32) + (added[:LV] + added[LV:])
            acc[p] = before
        return before

    total = jnp.zeros((LV, WIDE), F32)
    for part, (begin, end) in zip(copies, PARTS):
        wait_halo(part)
        total = lax.fori_loop(begin, end, spread, total)

    def place_gradient(y, j):
        w = 3 * y + j
        field[2, y + 1, :, WIDE * j:WIDE * j + WIDE] = acc[pair_ref[4, w]] * pair_ref[5, w].astype(F32)

    halo2 = []
    for j in range(3):
        for y in (0, ROWS - 1):
            place_gradient(y, j)
        halo2.append(halo_part(field.at[2], j, second_s, second_r))
    for y in INNER_FIRST[:6]:
        for j in range(3):
            place_gradient(y, j)
    solve(1, 1, 2, halo2, into_field(3))

    outs = []
    for v in range(VARS):
        rows = slice(LEVB * v, LEVB * v + LEVB)
        result = [stencil(3, y, v, 1) + field[0, y + 1, rows, :] for y in range(ROWS)]
        out_stage = inc_ref.at[v]
        out_stage[...] = jnp.swapaxes(jnp.stack(result), 0, 1)
        outs.append(pltpu.make_async_copy(out_stage, out_ref.at[:, v], out_sem.at[v]))
        outs[-1].start()
    for copy in outs:
        copy.wait()
    for copy in sent:
        copy.wait_send()


def shards(
    increment, courant_x, courant_y, level_inverse, coupling, profile, send_column, send_block, send_count, obs_weight,
):
    vmem = pl.BlockSpec(memory_space=pltpu.VMEM)
    any_space = pl.BlockSpec(memory_space=pl.ANY)
    smem = pl.BlockSpec(memory_space=pltpu.SMEM)
    dma = pltpu.SemaphoreType.DMA
    return pl.pallas_call(
        kernel,
        out_shape=jax.ShapeDtypeStruct(increment.shape, F32),
        in_specs=[any_space] * 3 + [vmem] * 5 + [smem] * 2,
        out_specs=any_space,
        scratch_shapes=[
            pltpu.VMEM((4, ROWS + 2, LV, NX), F32),
            pltpu.VMEM((ROWS + 2, LEVB, NX), F32),
            pltpu.VMEM((5, ROWS, LEVB, NX), F32),
            pltpu.VMEM((4, ROWS, LEVB, NX), F32),
            pltpu.VMEM((2, LV, NX), F32),
            pltpu.VMEM((2, ROWS, 12, 8, NX), F32),
            pltpu.VMEM((2, 3 * LV, NX), BF16),
            pltpu.VMEM((2, LV + 16, 3 * LV), BF16),
            pltpu.VMEM((2, 128, 128), F32),
            pltpu.VMEM((2, 2, LV, 128), F32),
            pltpu.VMEM((LV, 128), F32),
            pltpu.VMEM((12, 8, 128), F32),
            pltpu.VMEM((3, 8, 128), F32),
            pltpu.VMEM((2, 2, VARS * ROWS, NX), F32),
            pltpu.VMEM((2, 3, VARS * ROWS, NX), F32),
            pltpu.VMEM((2, 2, 11, 8, NX), F32),
            pltpu.VMEM((2, 2, 3, 8, NX), F32),
            pltpu.VMEM((4, 3, 8, 128), F32),
            pltpu.VMEM((64, 1, 128), F32),
            pltpu.VMEM((64, 128), F32),
            pltpu.VMEM((128, 128), F32),
            pltpu.VMEM((128, 128), jnp.int32),
            pltpu.VMEM((CHUNKS, 1, CHUNK), jnp.int32),
            pltpu.VMEM((CHUNKS, 1, CHUNK), F32),
            pltpu.VMEM((8, 128), jnp.int32),
            pltpu.VMEM((CHUNKS, LV, CHUNK), F32),
            pltpu.VMEM((WINDOWS, 2 * LV, WIDE), BF16),
            pltpu.VMEM((PAIRS, WIDE, CHUNK), BF16),
            pltpu.VMEM((PAIRS, 1, CHUNK), F32),
            pltpu.VMEM((3, PAIRS, 1, CHUNK), F32),
            pltpu.VMEM((PAIRS, LV, WIDE), F32),
            pltpu.VMEM((VARS, LEVB, ROWS, NX), F32),
            pltpu.VMEM((LEVB, ROWS, NX), F32),
            pltpu.VMEM((LEVB, ROWS, NX), F32),
            pltpu.SMEM((8, 128), jnp.int32),
            dma((2, 3)), dma((2, 3)), dma((2, 3)), dma((2, 3)), dma((2, 2, 3)), dma((2, 2, 3)), dma((2, 2, 3)), dma((2, 2, 3)),
            dma((2,)), dma((2,)), dma((3,)), dma((3,)),
            dma((2, 3, 2)), dma((2, 3, 2)), dma((4, 3)), dma((4, 3)), dma((TILES - 1,)), dma((TILES - 1,)),
            dma((3,)), dma((3,)),
            dma, dma((VARS,)), dma((VARS + 2,)),
        ],
        compiler_params=pltpu.CompilerParams(
            collective_id=0, has_side_effects=True, vmem_limit_bytes=56 * 1024 * 1024),
    )(
        increment, courant_x, courant_y, level_inverse, profile.transpose(1, 0, 2),
        send_column.reshape(64, 128), send_block.reshape(64, 128), obs_weight.reshape(64, 1, 128),
        coupling, send_count,
    )


def solution(mesh):
    return jax.shard_map(
        shards,
        mesh=mesh,
        in_specs=(
            P("band", None, "tile", None),
            P("band", "tile", None),
            P("band", "tile", None),
            P(None, "band", None),
            P(),
            P("band", None, None),
            P("tile", None),
            P("tile", None),
            P("tile", None),
            P("tile", None),
        ),
        out_specs=P("band", None, "tile", None),
        check_vma=False,
    )
```

```python
import functools

import jax
import jax.numpy as jnp
from jax import lax
from jax.experimental import pallas as pl
from jax.experimental.pallas import tpu as pltpu
from jax.sharding import PartitionSpec as P

MESH = pl.DeviceIdType.MESH
VARS = 5
LEVB = 16
LV = VARS * LEVB
ROWS = 8
NX = 768
BANDS = 4
TILES = 32
CHUNK = 256
CHUNKS = 32
WIDE = 256
WINDOWS = 24
PAIRS = 56
NBLK = 64
INNER_FIRST = (1, 2, 3, 4, 5, 6, 0, 7)
PARTS = ((0, 2), (2, 4), (4, 6), (6, 7))
SPLIT = 24
F32 = jnp.float32
BF16 = jnp.bfloat16


def halves(value):
    high = value.astype(BF16)
    low = (value - high.astype(F32)).astype(BF16)
    return high, low


def mm(a, b):
    return jnp.dot(a, b, preferred_element_type=F32)


def wide(value):
    return jnp.concatenate([value] * (NX // 128), axis=1)


def sort_pairs(keys, payload):
    shape = keys.shape
    slab, sub, lane = (lax.broadcasted_iota(jnp.int32, shape, axis) for axis in range(3))
    place = lane * 64 + sub * 8 + slab
    for k in range(1, 14):
        for j in range(k - 1, -1, -1):
            distance = 1 << j
            bit, block = (place >> j) & 1, (place >> k) & 1
            flip = bit != block
            if j < 3:
                def partner(x):
                    parts = x.reshape(8 >> (j + 1), 2, distance, 8, 128)
                    return jnp.concatenate([parts[:, 1:], parts[:, :1]], axis=1).reshape(shape)
            else:
                axis, step, size = (1, distance >> 3, 8) if j < 6 else (2, distance >> 6, 128)

                def partner(x):
                    if 2 * step == size:
                        return pltpu.roll(x, step, axis)
                    return jnp.where(bit == 1, pltpu.roll(x, step, axis), pltpu.roll(x, size - step, axis))
            other, other_payload = partner(keys), partner(payload)
            take = jnp.where(flip, (keys < other).astype(jnp.int32), (keys > other).astype(jnp.int32)) == 1
            keys = jnp.where(take, other, keys)
            payload = jnp.where(take, other_payload, payload)
    return keys, payload


def kernel(
    inc_hbm, cx_hbm, cy_hbm, inv_ref, prof_ref, column_ref, block_ref, weight_ref, coupling_ref, count_ref,
    out_ref,
    field, cyh, co, adj, partial, local, stack, mext, gm, cols, tab, tabl, tabr, edges, recv, beside, corner, coefs, wbuf, wrow, turn, turn_key, keyr, wgtr, pairv,
    ps, xs, onehot, val, valr, acc, inc_ref, cx_ref, cy_ref, pair_ref,
    first_s, first_r, second_s, second_r, halo_s, halo_r, diag_s, diag_r, cy_s, cy_r, cf_s, cf_r, ed_s, ed_r, va_s, va_r, wt_s, wt_r, tab_s, tab_r, pair_sem, out_sem, in_sem,
):
    band = lax.axis_index("band")
    tile = lax.axis_index("tile")
    north = lax.rem(tile + 1, TILES)
    south = lax.rem(tile + TILES - 1, TILES)
    partner = [lax.rem(band + o, BANDS) for o in (1, 2, 3)]

    barrier = pltpu.get_barrier_semaphore()
    for o in range(1, TILES):
        pl.semaphore_signal(
            barrier, inc=1, device_id={"tile": lax.rem(tile + o, TILES)}, device_id_type=MESH)
    for p in partner:
        pl.semaphore_signal(barrier, inc=1, device_id={"band": p}, device_id_type=MESH)
    for p in partner:
        for t in (north, south):
            pl.semaphore_signal(barrier, inc=1, device_id={"tile": t, "band": p}, device_id_type=MESH)

    sent = []

    def halo(buffer, send, receive):
        up = pltpu.make_async_remote_copy(
            buffer.at[ROWS], buffer.at[0], send.at[0], receive.at[0],
            device_id={"tile": north}, device_id_type=MESH)
        down = pltpu.make_async_remote_copy(
            buffer.at[1], buffer.at[ROWS + 1], send.at[1], receive.at[1],
            device_id={"tile": south}, device_id_type=MESH)
        up.start()
        down.start()
        sent.extend([up, down])
        return up, down

    def halo_part(buffer, c, send, receive):
        cols = slice(WIDE * c, WIDE * c + WIDE)
        pair = []
        for n, (source, target, place) in enumerate(((ROWS, north, 0), (1, south, ROWS + 1))):
            copy = pltpu.make_async_remote_copy(
                buffer.at[source, :, cols], buffer.at[place, :, cols], send.at[n, c], receive.at[n, c],
                device_id={"tile": target}, device_id_type=MESH)
            copy.start()
            pair.append(copy)
        sent.extend(pair)
        return pair

    def band_copy(source, target, send, receive, o):
        copy = pltpu.make_async_remote_copy(
            source, target, send, receive, device_id={"band": partner[o]}, device_id_type=MESH)
        copy.start()
        sent.append(copy)
        return copy

    loads = [pltpu.make_async_copy(inc_hbm.at[:, v], inc_ref.at[v], in_sem.at[v]) for v in range(VARS)]
    loads.append(pltpu.make_async_copy(cy_hbm, cy_ref, in_sem.at[VARS]))
    loads.append(pltpu.make_async_copy(cx_hbm, cx_ref, in_sem.at[VARS + 1]))
    for copy in loads:
        copy.start()

    gm[...] = jnp.zeros((2, 128, 128), F32)
    tab[...] = jnp.zeros((LV, 128), F32)
    for v in range(VARS):
        rows = slice(LEVB * v, LEVB * v + LEVB)
        gm[0, rows, rows] = inv_ref[v]
        tab[rows, 0:NBLK] = prof_ref[v]
    gm[1] = gm[0].T
    row_lane = lax.broadcasted_iota(jnp.int32, (8, 128), 1)

    def at_lanes(offset, factors):
        total = jnp.zeros((8, 128), F32)
        for v in range(VARS):
            total = total + jnp.where(row_lane == LEVB * v + offset, factors[v], 0.0)
        return total

    def rows_of(kind, offset):
        rows = [gm[kind, LEVB * v + offset:LEVB * v + offset + 1, :] for v in range(VARS)]
        if kind == 1:
            rows = [coupling_ref[v] * rows[v] for v in range(VARS)]
        return jnp.concatenate(rows + [jnp.zeros((3, 128), F32)], axis=0)

    ones = [1.0] * VARS
    scales = [coupling_ref[v] for v in range(VARS)]
    scale_first, scale_last = at_lanes(0, scales), at_lanes(LEVB - 1, scales)
    one_first, one_last = at_lanes(0, ones), at_lanes(LEVB - 1, ones)
    lasts = [rows_of(kind, LEVB - 1) for kind in range(2)]
    firsts = [rows_of(kind, 0) for kind in range(2)]

    def across(value, weight):
        return jnp.broadcast_to(jnp.sum(value * weight[0:1], axis=1, keepdims=True), (value.shape[0], 128))

    for v in range(VARS):
        loads[v].wait()
        turned = jnp.swapaxes(inc_ref[v], 0, 1)
        field[0, 1:ROWS + 1, LEVB * v:LEVB * v + LEVB, :] = turned
    coefs[0, 0] = across(firsts[0], scale_first)
    coefs[0, 1] = across(lasts[0], scale_first)
    coefs[0, 2] = across(firsts[0], scale_last)
    pl.semaphore_wait(barrier, TILES + BANDS - 2 + 2 * (BANDS - 1))
    halo1 = [halo_part(field.at[0], c, first_s, first_r) for c in range(3)]
    cf_copies = [
        band_copy(coefs.at[0], coefs.at[o + 1], cf_s.at[o], cf_r.at[o], o) for o in range(3)
    ]
    cols[0, 0] = across(gm[0, :LV], scale_first)
    cols[0, 1] = across(gm[0, :LV], scale_last)
    cols[1, 0] = across(gm[1, :LV], one_first)
    cols[1, 1] = across(gm[1, :LV], one_last)

    wt_copies = []
    for o in range(1, TILES):
        target = lax.rem(tile + o, TILES)
        copy = pltpu.make_async_remote_copy(
            weight_ref.at[pl.ds(2 * target, 2)], wbuf.at[pl.ds(2 * tile, 2)], wt_s.at[o - 1], wt_r.at[o - 1],
            device_id={"tile": target}, device_id_type=MESH)
        copy.start()
        sent.append(copy)
        wt_copies.append(copy)
    loads[VARS].wait()
    loads[VARS + 1].wait()
    cyh[1:ROWS + 1] = jnp.swapaxes(cy_ref[...], 0, 1)
    halo_cy = halo(cyh, cy_s, cy_r)
    co[0] = jnp.swapaxes(cx_ref[...], 0, 1)

    lane = lax.broadcasted_iota(jnp.int32, (LEVB, NX), 1)
    for y in range(ROWS):
        cx = co[0, y]
        cy = cyh[y + 1]
        ax, bx = (jnp.abs(cx) + cx) * 0.5, (jnp.abs(cx) - cx) * 0.5
        ay, by = (jnp.abs(cy) + cy) * 0.5, (jnp.abs(cy) - cy) * 0.5
        co[0, y] = 1.0 - ax - bx - ay - by
        co[1, y] = jnp.where(lane == 0, 0.0, ax)
        co[2, y] = jnp.where(lane == NX - 1, 0.0, bx)
        if y == 0:
            ay = jnp.where(tile == 0, 0.0, ay)
        if y == ROWS - 1:
            by = jnp.where(tile == TILES - 1, 0.0, by)
        co[3, y] = ay
        co[4, y] = by
        adj[0, y] = jnp.where(lane == 0, 0.0, pltpu.roll(bx, 1, 1))
        adj[1, y] = jnp.where(lane == NX - 1, 0.0, pltpu.roll(ax, NX - 1, 1))

    for copy in cf_copies:
        copy.wait_recv()

    def of_band(lane_index):
        result = []
        for j in range(BANDS):
            total = jnp.zeros((8, 128), F32)
            for b in range(BANDS):
                entry = coefs[(b - j) % BANDS, lane_index]
                total = total + jnp.where(band == b, entry, 0.0)
            result.append(total)
        return result

    def select(values):
        total = jnp.zeros((8, 128), F32)
        for b in range(BANDS):
            total = total + jnp.where(band == b, values[b], 0.0)
        return total

    k0, k15, g0 = of_band(0), of_band(1), of_band(2)
    zero = jnp.zeros((8, 128), F32)

    def chain(a, g):
        e = [zero] * (BANDS + 1)
        for j in range(BANDS - 1, -1, -1):
            e[j] = k0[j] + g[j] * e[j + 1] * a[j]
        into_first = select([g[b] * e[b + 1] for b in range(BANDS)])
        own = select([e[b + 1] for b in range(BANDS)])
        low, high = [], []
        for o in (1, 2, 3):
            t_list, s_list = [], []
            for b in range(BANDS):
                j = (b - o) % BANDS
                factor = zero + 1.0
                if j < b:
                    for k in range(j + 1, b):
                        factor = factor * a[k]
                    t_list.append(factor)
                    s_list.append(e[b + 1] * a[b] * factor)
                else:
                    for k in range(b + 1, j):
                        factor = factor * g[k]
                    t_list.append(zero)
                    s_list.append(factor)
            low.append(select(t_list))
            high.append(select(s_list))
        return into_first, own, low, high

    chains = (chain(k15, g0), chain(g0, k15))
    for kind in range(2):
        first = firsts[kind] + chains[kind][0] * lasts[kind]
        matrix = jnp.concatenate([gm[kind, :LV, :], lasts[kind], first], axis=0)[:, :LV]
        high, low = halves(matrix)
        mext[kind] = jnp.concatenate([high, high, low], axis=1)

    high, low = halves(tab[...])
    tabl[...] = mm(mext[1], jnp.concatenate([high, low, high], axis=0)).reshape(12, 8, 128)
    tab_copies = [
        band_copy(tabl.at[10 + (band + o + 1) // BANDS], tabr.at[o], tab_s.at[o], tab_r.at[o], o) for o in range(3)
    ]

    def stencil(src, y, v, kind, below=True, above=True):
        rows = slice(LEVB * v, LEVB * v + LEVB)
        f = field[src, y + 1, rows, :]
        west, east = pltpu.roll(f, 1, 1), pltpu.roll(f, NX - 1, 1)
        cw, ce = (co[1, y], co[2, y]) if kind == 0 else (adj[0, y], adj[1, y])
        result = co[0, y] * f + cw * west + ce * east
        if below:
            result = result + (co[3, y] if kind == 0 else adj[2, y]) * field[src, y, rows, :]
        if above:
            result = result + (co[4, y] if kind == 0 else adj[3, y]) * field[src, y + 2, rows, :]
        return result

    def solve(stage, kind, src, arrivals, store_row, inner, gap=None):
        copies, halos = [], []
        order = INNER_FIRST

        def multiply(y, k, slot, part_cols, value):
            for v in range(VARS):
                high, low = halves(value(v))
                for n, half in enumerate((high, low, high)):
                    stack[slot, LV * n + LEVB * v:LV * n + LEVB * v + LEVB, part_cols] = half
            result = mm(mext[kind], stack[slot, :, part_cols])
            local[stage, y, :, :, part_cols] = result.reshape(12, 8, result.shape[1])
            edges[stage, 0, VARS * k:VARS * k + VARS, part_cols] = result[LV:LV + VARS]
            edges[stage, 1, VARS * k:VARS * k + VARS, part_cols] = result[LV + 8:LV + 8 + VARS]

        def send_edges(part, lo, hi):
            for o in range(3):
                above = (band + o + 1) // BANDS
                copies.append(band_copy(
                    edges.at[stage, above, lo:hi], recv.at[stage, o, lo:hi],
                    ed_s.at[stage, o, part], ed_r.at[stage, o, part], o))

        for k, y in enumerate(order[:6]):
            multiply(y, k, k % 2, slice(0, NX), lambda v: stencil(src, y, v, kind))
            if k == 4:
                send_edges(0, 0, SPLIT)
        outer = ((0, 0, 1, south), (ROWS - 1, ROWS + 1, 0, north))
        for i, (y, beyond, side, target) in enumerate(outer):
            for v in range(VARS):
                partial[i, LEVB * v:LEVB * v + LEVB, :] = stencil(src, y, v, kind, y > 0, y == 0)
        for c in range(3):
            part_cols = slice(WIDE * c, WIDE * c + WIDE)
            wait_halo(arrivals[c])
            for i, (y, beyond, side, target) in enumerate(outer):
                factor = (co[3 + i, y, :, part_cols]) if kind == 0 else adj[2 + i, y, :, part_cols]

                def value(v):
                    rows = slice(LEVB * v, LEVB * v + LEVB)
                    return partial[i, rows, part_cols] + factor * field[src, beyond, rows, part_cols]

                multiply(y, 6 + i, i, part_cols, value)
                copy = pltpu.make_async_remote_copy(
                    local.at[stage, y, 0:11, :, part_cols], beside.at[stage, side, :, :, part_cols],
                    halo_s.at[stage, side, c], halo_r.at[stage, side, c],
                    device_id={"tile": target}, device_id_type=MESH)
                copy.start()
                halos.append(copy)
        send_edges(1, SPLIT, VARS * ROWS)
        for y, beyond, side, target in outer:
            for o in range(3):
                above = (band + o + 1) // BANDS
                copy = pltpu.make_async_remote_copy(
                    local.at[stage, y, 10 + above], corner.at[stage, side, o],
                    diag_s.at[stage, side, o], diag_r.at[stage, side, o],
                    device_id={"tile": target, "band": partner[o]}, device_id_type=MESH)
                copy.start()
                halos.append(copy)
        sent.extend(halos)
        if gap is not None:
            gap()
        _, own, low_c, high_c = chains[kind]

        def complete(y, mine, got, parts):
            t = jnp.zeros((VARS, NX), F32)
            s = wide(own[:VARS]) * mine
            for o in range(3):
                t = t + wide(low_c[o][:VARS]) * got[o]
                s = s + wide(high_c[o][:VARS]) * got[o]
            for v in range(VARS):
                rows = slice(LEVB * v, LEVB * v + LEVB)
                left, right = wide(cols[kind, 0, rows, :]), wide(cols[kind, 1, rows, :])
                store_row(y, v, parts(v) + left * t[v:v + 1] + right * s[v:v + 1])

        for copy in copies:
            copy.wait_recv()
        for k, y in enumerate(order):
            span = slice(VARS * k, VARS * k + VARS)
            complete(
                y, edges[stage, 0, span, :], [recv[stage, o, span, :] for o in range(3)],
                lambda v: local[stage, y, 2 * v:2 * v + 2].reshape(LEVB, NX))
        inner()
        for copy in halos:
            copy.wait_recv()
        for side, y in ((0, -1), (1, ROWS)):
            complete(
                y, beside[stage, side, 10][:VARS], [corner[stage, side, o][:VARS] for o in range(3)],
                lambda v: beside[stage, side, 2 * v:2 * v + 2].reshape(LEVB, NX))

    def wait_halo(copies):
        for copy in copies:
            copy.wait_recv()

    def into_field(index):
        def store(y, v, value):
            field[index, y + 1, LEVB * v:LEVB * v + LEVB, :] = value
        return store

    def store_state(y, v, value):
        high, low = halves(value)
        for j in range(3):
            cols = slice(WIDE * j, WIDE * j + WIDE)
            xs[3 * y + j, LEVB * v:LEVB * v + LEVB, :] = high[:, cols]
            xs[3 * y + j, LV + LEVB * v:LV + LEVB * v + LEVB, :] = low[:, cols]

    def sort_slots():
        for copy in wt_copies:
            copy.wait_recv()
        own = pl.ds(2 * tile, 2)
        wbuf[own] = weight_ref[own]
        slot = lax.broadcasted_iota(jnp.int32, (1, 128), 1)
        for r in range(64):
            live = slot < count_ref[0, r // 2] - 128 * (r % 2)
            wrow[r:r + 1, :] = jnp.where(live, wbuf[r], 0.0)
        keys = (column_ref[...] * NBLK + block_ref[...]).reshape(8, 8, 128)
        keys, weights = sort_pairs(keys, wrow[...].reshape(8, 8, 128))
        turn_key[0:64, :] = keys.reshape(64, 128)
        turn_key[64:128, :] = jnp.zeros((64, 128), jnp.int32)
        turn_key[...] = turn_key[...].T
        turn[0:64, :] = weights.reshape(64, 128)
        turn[64:128, :] = jnp.zeros((64, 128), F32)
        turn[...] = turn[...].T

        def rows_of_chunks(ref):
            return jnp.concatenate(
                [ref[pl.ds(q, CHUNKS, stride=4), :][:, :64] for q in range(4)], axis=1)

        rows, weights = rows_of_chunks(turn_key), rows_of_chunks(turn)
        for c in range(CHUNKS):
            keyr[c] = rows[c:c + 1]
            wgtr[c] = weights[c:c + 1]
        first = jnp.broadcast_to(rows[:, 0:1] // (NBLK * WIDE), (CHUNKS, 128))
        last = jnp.broadcast_to(rows[:, CHUNK - 1:CHUNK] // (NBLK * WIDE), (CHUNKS, 128))
        number = last - first + 1
        sub = lax.broadcasted_iota(jnp.int32, (CHUNKS, 128), 0)
        p = lax.broadcasted_iota(jnp.int32, (CHUNKS, 128), 1)
        upto = number
        for d in (1, 2, 4, 8, 16):
            upto = upto + jnp.where(sub >= d, pltpu.roll(upto, d, 0), 0)
        start = upto - number

        def down(value):
            return jnp.sum(value, axis=0, keepdims=True)

        chunk = jnp.clip(down(jnp.where(start <= p, 1, 0)) - 1, 0, CHUNKS - 1)
        window = down(jnp.where(sub == chunk, first - start + p, 0))
        valid = p[0:1] < upto[CHUNKS - 1:CHUNKS]
        index = jnp.clip(jnp.where(valid, window, WINDOWS - 1), 0, WINDOWS - 1)
        base = jnp.where(valid, window * WIDE, -(1 << 20))
        same = jnp.where((p[0:1] > 0) & (index == pltpu.roll(index, 1, 1)), 1, 0)
        latest = jnp.clip(down(jnp.clip(p - first + 1, 0, number)) - 1, 0, PAIRS - 1)
        some = jnp.minimum(down(jnp.where((first <= p) & (p <= last), 1, 0)), 1)
        zeros = jnp.zeros((2, 128), jnp.int32)
        pairv[...] = jnp.concatenate([chunk, index, base, same, latest, some, zeros], axis=0)
        copy = pltpu.make_async_copy(pairv, pair_ref, pair_sem)
        copy.start()
        copy.wait()

    def pick_slots():
        for copy in tab_copies:
            copy.wait_recv()
        _, own, low_c, high_c = chains[1]
        t = jnp.zeros((8, 128), F32)
        s = own * tabl[10]
        for o in range(3):
            t = t + low_c[o] * tabr[o]
            s = s + high_c[o] * tabr[o]
        for v in range(VARS):
            rows = slice(LEVB * v, LEVB * v + LEVB)
            tab[rows, :] = (
                tabl[2 * v:2 * v + 2].reshape(LEVB, 128)
                + cols[1, 0, rows, :] * t[v:v + 1] + cols[1, 1, rows, :] * s[v:v + 1])
        profiles = jnp.concatenate(halves(tab[:, 0:NBLK]), axis=0)
        block_iota = lax.broadcasted_iota(jnp.int32, (NBLK, CHUNK), 0)
        cell_iota = lax.broadcasted_iota(jnp.int32, (WIDE, CHUNK), 0)

        def pick_profiles(i, carry):
            for u in range(4):
                c = 4 * i + u
                picked = mm(profiles, (block_iota == keyr[c] % NBLK).astype(BF16))
                ps[c] = picked[:LV] + picked[LV:]
            return carry

        lax.fori_loop(0, CHUNKS // 4, pick_profiles, 0)

        def pick_cells(i, carry):
            for u in range(4):
                p = 4 * i + u
                onehot[p] = (cell_iota == keyr[pair_ref[0, p]] // NBLK - pair_ref[2, p]).astype(BF16)
            return carry

        lax.fori_loop(0, PAIRS // 4, pick_cells, 0)

    def gap():
        sort_slots()
        pick_slots()

    def observe_rows(rows):
        for y in rows:
            for v in range(VARS):
                store_state(y, v, stencil(1, y, v, 0))

    solve(0, 0, 0, halo1, into_field(1), lambda: observe_rows(INNER_FIRST[:6]), gap)
    observe_rows(INNER_FIRST[6:])

    def observe(i, carry):
        for u in range(8):
            p = 8 * i + u
            picked = mm(xs[pair_ref[1, p]], onehot[p])
            product = (picked[:LV] + picked[LV:]) * ps[pair_ref[0, p]]
            val[p] = jnp.sum(product, axis=0, keepdims=True)
        return carry

    copies = []
    for n, (begin, end) in enumerate(PARTS):
        lax.fori_loop(begin, end, observe, 0)
        span = slice(8 * begin, 8 * end)
        copies.append([
            band_copy(val.at[span], valr.at[o, span], va_s.at[n, o], va_r.at[n, o], o) for o in range(3)])

    wait_halo(halo_cy)
    for y in range(ROWS):
        below, above = cyh[y], cyh[y + 2]
        by = (jnp.abs(below) - below) * 0.5
        ay = (jnp.abs(above) + above) * 0.5
        if y == 0:
            by = jnp.where(tile == 0, 0.0, by)
        if y == ROWS - 1:
            ay = jnp.where(tile == TILES - 1, 0.0, ay)
        adj[2, y] = by
        adj[3, y] = ay
    def spread(i, before):
        for u in range(8):
            p = 8 * i + u
            c = pair_ref[0, p]
            values = (val[p] + valr[0, p]) + (valr[1, p] + valr[2, p])
            high, low = halves(ps[c] * (values * wgtr[c]))
            both = jnp.concatenate([high, low], axis=0)
            added = lax.dot_general(
                both, onehot[p], (((1,), (1,)), ((), ())), preferred_element_type=F32)
            before = before * pair_ref[3, p].astype(F32) + (added[:LV] + added[LV:])
            acc[p] = before
        return before

    total = jnp.zeros((LV, WIDE), F32)
    for part, (begin, end) in zip(copies, PARTS):
        wait_halo(part)
        total = lax.fori_loop(begin, end, spread, total)

    def place_gradient(y, j):
        w = 3 * y + j
        field[2, y + 1, :, WIDE * j:WIDE * j + WIDE] = acc[pair_ref[4, w]] * pair_ref[5, w].astype(F32)

    halo2 = []
    for j in range(3):
        for y in (0, ROWS - 1):
            place_gradient(y, j)
        halo2.append(halo_part(field.at[2], j, second_s, second_r))
    for y in INNER_FIRST[:6]:
        for j in range(3):
            place_gradient(y, j)
    def finish(y, v):
        rows = slice(LEVB * v, LEVB * v + LEVB)
        field[1, y + 1, rows, :] = stencil(3, y, v, 1) + field[0, y + 1, rows, :]

    def finish_inner():
        for y in INNER_FIRST[:6]:
            for v in range(VARS):
                finish(y, v)

    solve(1, 1, 2, halo2, into_field(3), finish_inner)
    outs = []
    for v in range(VARS):
        for y in INNER_FIRST[6:]:
            finish(y, v)
        out_stage = inc_ref.at[v]
        out_stage[...] = jnp.swapaxes(field[1, 1:ROWS + 1, LEVB * v:LEVB * v + LEVB, :], 0, 1)
        outs.append(pltpu.make_async_copy(out_stage, out_ref.at[:, v], out_sem.at[v]))
        outs[-1].start()
    for copy in outs:
        copy.wait()
    for copy in sent:
        copy.wait_send()


def shards(
    increment, courant_x, courant_y, level_inverse, coupling, profile, send_column, send_block, send_count, obs_weight,
):
    vmem = pl.BlockSpec(memory_space=pltpu.VMEM)
    any_space = pl.BlockSpec(memory_space=pl.ANY)
    smem = pl.BlockSpec(memory_space=pltpu.SMEM)
    dma = pltpu.SemaphoreType.DMA
    return pl.pallas_call(
        kernel,
        out_shape=jax.ShapeDtypeStruct(increment.shape, F32),
        in_specs=[any_space] * 3 + [vmem] * 5 + [smem] * 2,
        out_specs=any_space,
        scratch_shapes=[
            pltpu.VMEM((4, ROWS + 2, LV, NX), F32),
            pltpu.VMEM((ROWS + 2, LEVB, NX), F32),
            pltpu.VMEM((5, ROWS, LEVB, NX), F32),
            pltpu.VMEM((4, ROWS, LEVB, NX), F32),
            pltpu.VMEM((2, LV, NX), F32),
            pltpu.VMEM((2, ROWS, 12, 8, NX), F32),
            pltpu.VMEM((2, 3 * LV, NX), BF16),
            pltpu.VMEM((2, LV + 16, 3 * LV), BF16),
            pltpu.VMEM((2, 128, 128), F32),
            pltpu.VMEM((2, 2, LV, 128), F32),
            pltpu.VMEM((LV, 128), F32),
            pltpu.VMEM((12, 8, 128), F32),
            pltpu.VMEM((3, 8, 128), F32),
            pltpu.VMEM((2, 2, VARS * ROWS, NX), F32),
            pltpu.VMEM((2, 3, VARS * ROWS, NX), F32),
            pltpu.VMEM((2, 2, 11, 8, NX), F32),
            pltpu.VMEM((2, 2, 3, 8, NX), F32),
            pltpu.VMEM((4, 3, 8, 128), F32),
            pltpu.VMEM((64, 1, 128), F32),
            pltpu.VMEM((64, 128), F32),
            pltpu.VMEM((128, 128), F32),
            pltpu.VMEM((128, 128), jnp.int32),
            pltpu.VMEM((CHUNKS, 1, CHUNK), jnp.int32),
            pltpu.VMEM((CHUNKS, 1, CHUNK), F32),
            pltpu.VMEM((8, 128), jnp.int32),
            pltpu.VMEM((CHUNKS, LV, CHUNK), F32),
            pltpu.VMEM((WINDOWS, 2 * LV, WIDE), BF16),
            pltpu.VMEM((PAIRS, WIDE, CHUNK), BF16),
            pltpu.VMEM((PAIRS, 1, CHUNK), F32),
            pltpu.VMEM((3, PAIRS, 1, CHUNK), F32),
            pltpu.VMEM((PAIRS, LV, WIDE), F32),
            pltpu.VMEM((VARS, LEVB, ROWS, NX), F32),
            pltpu.VMEM((LEVB, ROWS, NX), F32),
            pltpu.VMEM((LEVB, ROWS, NX), F32),
            pltpu.SMEM((8, 128), jnp.int32),
            dma((2, 3)), dma((2, 3)), dma((2, 3)), dma((2, 3)), dma((2, 2, 3)), dma((2, 2, 3)), dma((2, 2, 3)), dma((2, 2, 3)),
            dma((2,)), dma((2,)), dma((3,)), dma((3,)),
            dma((2, 3, 2)), dma((2, 3, 2)), dma((4, 3)), dma((4, 3)), dma((TILES - 1,)), dma((TILES - 1,)),
            dma((3,)), dma((3,)),
            dma, dma((VARS,)), dma((VARS + 2,)),
        ],
        compiler_params=pltpu.CompilerParams(
            collective_id=0, has_side_effects=True, vmem_limit_bytes=56 * 1024 * 1024),
    )(
        increment, courant_x, courant_y, level_inverse, profile.transpose(1, 0, 2),
        send_column.reshape(64, 128), send_block.reshape(64, 128), obs_weight.reshape(64, 1, 128),
        coupling, send_count,
    )


def solution(mesh):
    return jax.shard_map(
        shards,
        mesh=mesh,
        in_specs=(
            P("band", None, "tile", None),
            P("band", "tile", None),
            P("band", "tile", None),
            P(None, "band", None),
            P(),
            P("band", None, None),
            P("tile", None),
            P("tile", None),
            P("tile", None),
            P("tile", None),
        ),
        out_specs=P("band", None, "tile", None),
        check_vma=False,
    )
```

```python
import functools

import jax
import jax.numpy as jnp
from jax import lax
from jax.experimental import pallas as pl
from jax.experimental.pallas import tpu as pltpu
from jax.sharding import PartitionSpec as P

MESH = pl.DeviceIdType.MESH
VARS = 5
LEVB = 16
LV = VARS * LEVB
ROWS = 8
NX = 768
BANDS = 4
TILES = 32
CHUNK = 256
CHUNKS = 32
WIDE = 256
WINDOWS = 24
PAIRS = 56
NBLK = 64
INNER_FIRST = (1, 2, 3, 4, 5, 6, 0, 7)
PARTS = ((0, 1), (1, 2), (2, 3), (3, 4))
SPLIT = 24
F32 = jnp.float32
BF16 = jnp.bfloat16


def halves(value):
    high = value.astype(BF16)
    low = (value - high.astype(F32)).astype(BF16)
    return high, low


def mm(a, b):
    return jnp.dot(a, b, preferred_element_type=F32)


def wide(value):
    return jnp.concatenate([value] * (NX // 128), axis=1)


def sort_pairs(keys, payload):
    shape = keys.shape
    slab, sub, lane = (lax.broadcasted_iota(jnp.int32, shape, axis) for axis in range(3))
    place = lane * 64 + sub * 8 + slab
    for k in range(1, 14):
        for j in range(k - 1, -1, -1):
            distance = 1 << j
            bit, block = (place >> j) & 1, (place >> k) & 1
            flip = bit != block
            if j < 3:
                def partner(x):
                    parts = x.reshape(8 >> (j + 1), 2, distance, 8, 128)
                    return jnp.concatenate([parts[:, 1:], parts[:, :1]], axis=1).reshape(shape)
            else:
                axis, step, size = (1, distance >> 3, 8) if j < 6 else (2, distance >> 6, 128)

                def partner(x):
                    if 2 * step == size:
                        return pltpu.roll(x, step, axis)
                    return jnp.where(bit == 1, pltpu.roll(x, step, axis), pltpu.roll(x, size - step, axis))
            other, other_payload = partner(keys), partner(payload)
            take = jnp.where(flip, (keys < other).astype(jnp.int32), (keys > other).astype(jnp.int32)) == 1
            keys = jnp.where(take, other, keys)
            payload = jnp.where(take, other_payload, payload)
    return keys, payload


def kernel(
    inc_hbm, cx_hbm, cy_hbm, inv_ref, prof_ref, column_ref, block_ref, weight_ref, coupling_ref, count_ref,
    out_ref,
    field, cyh, co, adj, partial, local, stack, mext, gm, cols, tab, tabl, tabr, edges, recv, beside, corner, coefs, wbuf, wrow, turn, turn_key, keyr, wgtr, pairv,
    ps, xs, onehot, val, valr, acc, inc_ref, cx_ref, cy_ref, pair_ref,
    first_s, first_r, second_s, second_r, halo_s, halo_r, diag_s, diag_r, cy_s, cy_r, cf_s, cf_r, ed_s, ed_r, va_s, va_r, wt_s, wt_r, tab_s, tab_r, pair_sem, out_sem, in_sem,
):
    band = lax.axis_index("band")
    tile = lax.axis_index("tile")
    north = lax.rem(tile + 1, TILES)
    south = lax.rem(tile + TILES - 1, TILES)
    partner = [lax.rem(band + o, BANDS) for o in (1, 2, 3)]

    barrier = pltpu.get_barrier_semaphore()
    for o in range(1, TILES):
        pl.semaphore_signal(
            barrier, inc=1, device_id={"tile": lax.rem(tile + o, TILES)}, device_id_type=MESH)
    for p in partner:
        pl.semaphore_signal(barrier, inc=1, device_id={"band": p}, device_id_type=MESH)
    for p in partner:
        for t in (north, south):
            pl.semaphore_signal(barrier, inc=1, device_id={"tile": t, "band": p}, device_id_type=MESH)

    sent = []

    def halo(buffer, send, receive):
        up = pltpu.make_async_remote_copy(
            buffer.at[ROWS], buffer.at[0], send.at[0], receive.at[0],
            device_id={"tile": north}, device_id_type=MESH)
        down = pltpu.make_async_remote_copy(
            buffer.at[1], buffer.at[ROWS + 1], send.at[1], receive.at[1],
            device_id={"tile": south}, device_id_type=MESH)
        up.start()
        down.start()
        sent.extend([up, down])
        return up, down

    def halo_part(buffer, c, send, receive):
        cols = slice(WIDE * c, WIDE * c + WIDE)
        pair = []
        for n, (source, target, place) in enumerate(((ROWS, north, 0), (1, south, ROWS + 1))):
            copy = pltpu.make_async_remote_copy(
                buffer.at[source, :, cols], buffer.at[place, :, cols], send.at[n, c], receive.at[n, c],
                device_id={"tile": target}, device_id_type=MESH)
            copy.start()
            pair.append(copy)
        sent.extend(pair)
        return pair

    def band_copy(source, target, send, receive, o):
        copy = pltpu.make_async_remote_copy(
            source, target, send, receive, device_id={"band": partner[o]}, device_id_type=MESH)
        copy.start()
        sent.append(copy)
        return copy

    loads = [pltpu.make_async_copy(inc_hbm.at[:, v], inc_ref.at[v], in_sem.at[v]) for v in range(VARS)]
    loads.append(pltpu.make_async_copy(cy_hbm, cy_ref, in_sem.at[VARS]))
    loads.append(pltpu.make_async_copy(cx_hbm, cx_ref, in_sem.at[VARS + 1]))
    for copy in loads:
        copy.start()

    gm[...] = jnp.zeros((2, 128, 128), F32)
    tab[...] = jnp.zeros((LV, 128), F32)
    for v in range(VARS):
        rows = slice(LEVB * v, LEVB * v + LEVB)
        gm[0, rows, rows] = inv_ref[v]
        tab[rows, 0:NBLK] = prof_ref[v]
    gm[1] = gm[0].T
    row_lane = lax.broadcasted_iota(jnp.int32, (8, 128), 1)

    def at_lanes(offset, factors):
        total = jnp.zeros((8, 128), F32)
        for v in range(VARS):
            total = total + jnp.where(row_lane == LEVB * v + offset, factors[v], 0.0)
        return total

    def rows_of(kind, offset):
        rows = [gm[kind, LEVB * v + offset:LEVB * v + offset + 1, :] for v in range(VARS)]
        if kind == 1:
            rows = [coupling_ref[v] * rows[v] for v in range(VARS)]
        return jnp.concatenate(rows + [jnp.zeros((3, 128), F32)], axis=0)

    ones = [1.0] * VARS
    scales = [coupling_ref[v] for v in range(VARS)]
    scale_first, scale_last = at_lanes(0, scales), at_lanes(LEVB - 1, scales)
    one_first, one_last = at_lanes(0, ones), at_lanes(LEVB - 1, ones)
    lasts = [rows_of(kind, LEVB - 1) for kind in range(2)]
    firsts = [rows_of(kind, 0) for kind in range(2)]

    def across(value, weight):
        return jnp.broadcast_to(jnp.sum(value * weight[0:1], axis=1, keepdims=True), (value.shape[0], 128))

    for v in range(VARS):
        loads[v].wait()
        turned = jnp.swapaxes(inc_ref[v], 0, 1)
        field[0, 1:ROWS + 1, LEVB * v:LEVB * v + LEVB, :] = turned
    coefs[0, 0] = across(firsts[0], scale_first)
    coefs[0, 1] = across(lasts[0], scale_first)
    coefs[0, 2] = across(firsts[0], scale_last)
    pl.semaphore_wait(barrier, TILES + BANDS - 2 + 2 * (BANDS - 1))
    halo1 = [halo_part(field.at[0], c, first_s, first_r) for c in range(3)]
    cf_copies = [
        band_copy(coefs.at[0], coefs.at[o + 1], cf_s.at[o], cf_r.at[o], o) for o in range(3)
    ]
    cols[0, 0] = across(gm[0, :LV], scale_first)
    cols[0, 1] = across(gm[0, :LV], scale_last)
    cols[1, 0] = across(gm[1, :LV], one_first)
    cols[1, 1] = across(gm[1, :LV], one_last)

    wt_copies = []
    for o in range(1, TILES):
        target = lax.rem(tile + o, TILES)
        copy = pltpu.make_async_remote_copy(
            weight_ref.at[pl.ds(2 * target, 2)], wbuf.at[pl.ds(2 * tile, 2)], wt_s.at[o - 1], wt_r.at[o - 1],
            device_id={"tile": target}, device_id_type=MESH)
        copy.start()
        sent.append(copy)
        wt_copies.append(copy)
    loads[VARS].wait()
    loads[VARS + 1].wait()
    cyh[1:ROWS + 1] = jnp.swapaxes(cy_ref[...], 0, 1)
    halo_cy = halo(cyh, cy_s, cy_r)
    co[0] = jnp.swapaxes(cx_ref[...], 0, 1)

    lane = lax.broadcasted_iota(jnp.int32, (LEVB, NX), 1)
    for y in range(ROWS):
        cx = co[0, y]
        cy = cyh[y + 1]
        ax, bx = (jnp.abs(cx) + cx) * 0.5, (jnp.abs(cx) - cx) * 0.5
        ay, by = (jnp.abs(cy) + cy) * 0.5, (jnp.abs(cy) - cy) * 0.5
        co[0, y] = 1.0 - ax - bx - ay - by
        co[1, y] = jnp.where(lane == 0, 0.0, ax)
        co[2, y] = jnp.where(lane == NX - 1, 0.0, bx)
        if y == 0:
            ay = jnp.where(tile == 0, 0.0, ay)
        if y == ROWS - 1:
            by = jnp.where(tile == TILES - 1, 0.0, by)
        co[3, y] = ay
        co[4, y] = by
        adj[0, y] = jnp.where(lane == 0, 0.0, pltpu.roll(bx, 1, 1))
        adj[1, y] = jnp.where(lane == NX - 1, 0.0, pltpu.roll(ax, NX - 1, 1))

    for copy in cf_copies:
        copy.wait_recv()

    def of_band(lane_index):
        result = []
        for j in range(BANDS):
            total = jnp.zeros((8, 128), F32)
            for b in range(BANDS):
                entry = coefs[(b - j) % BANDS, lane_index]
                total = total + jnp.where(band == b, entry, 0.0)
            result.append(total)
        return result

    def select(values):
        total = jnp.zeros((8, 128), F32)
        for b in range(BANDS):
            total = total + jnp.where(band == b, values[b], 0.0)
        return total

    k0, k15, g0 = of_band(0), of_band(1), of_band(2)
    zero = jnp.zeros((8, 128), F32)

    def chain(a, g):
        e = [zero] * (BANDS + 1)
        for j in range(BANDS - 1, -1, -1):
            e[j] = k0[j] + g[j] * e[j + 1] * a[j]
        into_first = select([g[b] * e[b + 1] for b in range(BANDS)])
        own = select([e[b + 1] for b in range(BANDS)])
        low, high = [], []
        for o in (1, 2, 3):
            t_list, s_list = [], []
            for b in range(BANDS):
                j = (b - o) % BANDS
                factor = zero + 1.0
                if j < b:
                    for k in range(j + 1, b):
                        factor = factor * a[k]
                    t_list.append(factor)
                    s_list.append(e[b + 1] * a[b] * factor)
                else:
                    for k in range(b + 1, j):
                        factor = factor * g[k]
                    t_list.append(zero)
                    s_list.append(factor)
            low.append(select(t_list))
            high.append(select(s_list))
        return into_first, own, low, high

    chains = (chain(k15, g0), chain(g0, k15))
    for kind in range(2):
        first = firsts[kind] + chains[kind][0] * lasts[kind]
        matrix = jnp.concatenate([gm[kind, :LV, :], lasts[kind], first], axis=0)[:, :LV]
        high, low = halves(matrix)
        mext[kind] = jnp.concatenate([high, high, low], axis=1)

    high, low = halves(tab[...])
    tabl[...] = mm(mext[1], jnp.concatenate([high, low, high], axis=0)).reshape(12, 8, 128)
    tab_copies = [
        band_copy(tabl.at[10 + (band + o + 1) // BANDS], tabr.at[o], tab_s.at[o], tab_r.at[o], o) for o in range(3)
    ]

    def stencil(src, y, v, kind, below=True, above=True):
        rows = slice(LEVB * v, LEVB * v + LEVB)
        f = field[src, y + 1, rows, :]
        west, east = pltpu.roll(f, 1, 1), pltpu.roll(f, NX - 1, 1)
        cw, ce = (co[1, y], co[2, y]) if kind == 0 else (adj[0, y], adj[1, y])
        result = co[0, y] * f + cw * west + ce * east
        if below:
            result = result + (co[3, y] if kind == 0 else adj[2, y]) * field[src, y, rows, :]
        if above:
            result = result + (co[4, y] if kind == 0 else adj[3, y]) * field[src, y + 2, rows, :]
        return result

    def solve(stage, kind, src, arrivals, store_row, inner, gap=None):
        copies, halos = [], []
        order = INNER_FIRST

        def multiply(y, k, slot, part_cols, value):
            for v in range(VARS):
                high, low = halves(value(v))
                for n, half in enumerate((high, low, high)):
                    stack[slot, LV * n + LEVB * v:LV * n + LEVB * v + LEVB, part_cols] = half
            result = mm(mext[kind], stack[slot, :, part_cols])
            local[stage, y, :, :, part_cols] = result.reshape(12, 8, result.shape[1])
            edges[stage, 0, VARS * k:VARS * k + VARS, part_cols] = result[LV:LV + VARS]
            edges[stage, 1, VARS * k:VARS * k + VARS, part_cols] = result[LV + 8:LV + 8 + VARS]

        def send_edges(part, lo, hi):
            for o in range(3):
                above = (band + o + 1) // BANDS
                copies.append(band_copy(
                    edges.at[stage, above, lo:hi], recv.at[stage, o, lo:hi],
                    ed_s.at[stage, o, part], ed_r.at[stage, o, part], o))

        for k, y in enumerate(order[:6]):
            multiply(y, k, k % 2, slice(0, NX), lambda v: stencil(src, y, v, kind))
            if k == 4:
                send_edges(0, 0, SPLIT)
        outer = ((0, 0, 1, south), (ROWS - 1, ROWS + 1, 0, north))
        for i, (y, beyond, side, target) in enumerate(outer):
            for v in range(VARS):
                partial[i, LEVB * v:LEVB * v + LEVB, :] = stencil(src, y, v, kind, y > 0, y == 0)
        for c in range(3):
            part_cols = slice(WIDE * c, WIDE * c + WIDE)
            wait_halo(arrivals[c])
            for i, (y, beyond, side, target) in enumerate(outer):
                factor = (co[3 + i, y, :, part_cols]) if kind == 0 else adj[2 + i, y, :, part_cols]

                def value(v):
                    rows = slice(LEVB * v, LEVB * v + LEVB)
                    return partial[i, rows, part_cols] + factor * field[src, beyond, rows, part_cols]

                multiply(y, 6 + i, i, part_cols, value)
                copy = pltpu.make_async_remote_copy(
                    local.at[stage, y, 0:11, :, part_cols], beside.at[stage, side, :, :, part_cols],
                    halo_s.at[stage, side, c], halo_r.at[stage, side, c],
                    device_id={"tile": target}, device_id_type=MESH)
                copy.start()
                halos.append(copy)
        send_edges(1, SPLIT, VARS * ROWS)
        for y, beyond, side, target in outer:
            for o in range(3):
                above = (band + o + 1) // BANDS
                copy = pltpu.make_async_remote_copy(
                    local.at[stage, y, 10 + above], corner.at[stage, side, o],
                    diag_s.at[stage, side, o], diag_r.at[stage, side, o],
                    device_id={"tile": target, "band": partner[o]}, device_id_type=MESH)
                copy.start()
                halos.append(copy)
        sent.extend(halos)
        if gap is not None:
            gap()
        _, own, low_c, high_c = chains[kind]

        def complete(y, mine, got, parts):
            t = jnp.zeros((VARS, NX), F32)
            s = wide(own[:VARS]) * mine
            for o in range(3):
                t = t + wide(low_c[o][:VARS]) * got[o]
                s = s + wide(high_c[o][:VARS]) * got[o]
            for v in range(VARS):
                rows = slice(LEVB * v, LEVB * v + LEVB)
                left, right = wide(cols[kind, 0, rows, :]), wide(cols[kind, 1, rows, :])
                store_row(y, v, parts(v) + left * t[v:v + 1] + right * s[v:v + 1])

        for copy in copies:
            copy.wait_recv()
        for k, y in enumerate(order):
            span = slice(VARS * k, VARS * k + VARS)
            complete(
                y, edges[stage, 0, span, :], [recv[stage, o, span, :] for o in range(3)],
                lambda v: local[stage, y, 2 * v:2 * v + 2].reshape(LEVB, NX))
        inner()
        for copy in halos:
            copy.wait_recv()
        for side, y in ((0, -1), (1, ROWS)):
            complete(
                y, beside[stage, side, 10][:VARS], [corner[stage, side, o][:VARS] for o in range(3)],
                lambda v: beside[stage, side, 2 * v:2 * v + 2].reshape(LEVB, NX))

    def wait_halo(copies):
        for copy in copies:
            copy.wait_recv()

    def into_field(index):
        def store(y, v, value):
            field[index, y + 1, LEVB * v:LEVB * v + LEVB, :] = value
        return store

    def store_state(y, v, value):
        high, low = halves(value)
        for j in range(3):
            cols = slice(WIDE * j, WIDE * j + WIDE)
            xs[3 * y + j, LEVB * v:LEVB * v + LEVB, :] = high[:, cols]
            xs[3 * y + j, LV + LEVB * v:LV + LEVB * v + LEVB, :] = low[:, cols]

    def sort_slots():
        for copy in wt_copies:
            copy.wait_recv()
        own = pl.ds(2 * tile, 2)
        wbuf[own] = weight_ref[own]
        slot = lax.broadcasted_iota(jnp.int32, (1, 128), 1)
        for r in range(64):
            live = slot < count_ref[0, r // 2] - 128 * (r % 2)
            wrow[r:r + 1, :] = jnp.where(live, wbuf[r], 0.0)
        keys = (column_ref[...] * NBLK + block_ref[...]).reshape(8, 8, 128)
        keys, weights = sort_pairs(keys, wrow[...].reshape(8, 8, 128))
        turn_key[0:64, :] = keys.reshape(64, 128)
        turn_key[64:128, :] = jnp.zeros((64, 128), jnp.int32)
        turn_key[...] = turn_key[...].T
        turn[0:64, :] = weights.reshape(64, 128)
        turn[64:128, :] = jnp.zeros((64, 128), F32)
        turn[...] = turn[...].T

        def rows_of_chunks(ref):
            return jnp.concatenate(
                [ref[pl.ds(q, CHUNKS, stride=4), :][:, :64] for q in range(4)], axis=1)

        rows, weights = rows_of_chunks(turn_key), rows_of_chunks(turn)
        for c in range(CHUNKS):
            keyr[c] = rows[c:c + 1]
            wgtr[c] = weights[c:c + 1]
        first = jnp.broadcast_to(rows[:, 0:1] // (NBLK * WIDE), (CHUNKS, 128))
        last = jnp.broadcast_to(rows[:, CHUNK - 1:CHUNK] // (NBLK * WIDE), (CHUNKS, 128))
        number = last - first + 1
        sub = lax.broadcasted_iota(jnp.int32, (CHUNKS, 128), 0)
        p = lax.broadcasted_iota(jnp.int32, (CHUNKS, 128), 1)
        upto = number
        for d in (1, 2, 4, 8, 16):
            upto = upto + jnp.where(sub >= d, pltpu.roll(upto, d, 0), 0)
        start = upto - number

        def down(value):
            return jnp.sum(value, axis=0, keepdims=True)

        chunk = jnp.clip(down(jnp.where(start <= p, 1, 0)) - 1, 0, CHUNKS - 1)
        window = down(jnp.where(sub == chunk, first - start + p, 0))
        valid = p[0:1] < upto[CHUNKS - 1:CHUNKS]
        index = jnp.clip(jnp.where(valid, window, WINDOWS - 1), 0, WINDOWS - 1)
        base = jnp.where(valid, window * WIDE, -(1 << 20))
        same = jnp.where((p[0:1] > 0) & (index == pltpu.roll(index, 1, 1)), 1, 0)
        latest = jnp.clip(down(jnp.clip(p - first + 1, 0, number)) - 1, 0, PAIRS - 1)
        some = jnp.minimum(down(jnp.where((first <= p) & (p <= last), 1, 0)), 1)
        zeros = jnp.zeros((2, 128), jnp.int32)
        pairv[...] = jnp.concatenate([chunk, index, base, same, latest, some, zeros], axis=0)
        copy = pltpu.make_async_copy(pairv, pair_ref, pair_sem)
        copy.start()
        copy.wait()

    def pick_slots():
        for copy in tab_copies:
            copy.wait_recv()
        _, own, low_c, high_c = chains[1]
        t = jnp.zeros((8, 128), F32)
        s = own * tabl[10]
        for o in range(3):
            t = t + low_c[o] * tabr[o]
            s = s + high_c[o] * tabr[o]
        for v in range(VARS):
            rows = slice(LEVB * v, LEVB * v + LEVB)
            tab[rows, :] = (
                tabl[2 * v:2 * v + 2].reshape(LEVB, 128)
                + cols[1, 0, rows, :] * t[v:v + 1] + cols[1, 1, rows, :] * s[v:v + 1])
        profiles = jnp.concatenate(halves(tab[:, 0:NBLK]), axis=0)
        block_iota = lax.broadcasted_iota(jnp.int32, (NBLK, CHUNK), 0)
        cell_iota = lax.broadcasted_iota(jnp.int32, (WIDE, CHUNK), 0)

        def pick_profiles(i, carry):
            for u in range(8):
                c = 8 * i + u
                picked = mm(profiles, (block_iota == keyr[c] % NBLK).astype(BF16))
                ps[c] = picked[:LV] + picked[LV:]
            return carry

        lax.fori_loop(0, CHUNKS // 8, pick_profiles, 0)

        def pick_cells(i, carry):
            for u in range(8):
                p = 8 * i + u
                onehot[p] = (cell_iota == keyr[pair_ref[0, p]] // NBLK - pair_ref[2, p]).astype(BF16)
            return carry

        lax.fori_loop(0, PAIRS // 8, pick_cells, 0)

    def gap():
        sort_slots()
        pick_slots()

    def observe_rows(rows):
        for y in rows:
            for v in range(VARS):
                store_state(y, v, stencil(1, y, v, 0))

    solve(0, 0, 0, halo1, into_field(1), lambda: observe_rows(INNER_FIRST[:6]), gap)
    observe_rows(INNER_FIRST[6:])

    def observe(i, carry):
        for u in range(14):
            p = 14 * i + u
            picked = mm(xs[pair_ref[1, p]], onehot[p])
            product = (picked[:LV] + picked[LV:]) * ps[pair_ref[0, p]]
            val[p] = jnp.sum(product, axis=0, keepdims=True)
        return carry

    copies = []
    for n, (begin, end) in enumerate(PARTS):
        lax.fori_loop(begin, end, observe, 0)
        span = slice(14 * begin, 14 * end)
        copies.append([
            band_copy(val.at[span], valr.at[o, span], va_s.at[n, o], va_r.at[n, o], o) for o in range(3)])

    wait_halo(halo_cy)
    for y in range(ROWS):
        below, above = cyh[y], cyh[y + 2]
        by = (jnp.abs(below) - below) * 0.5
        ay = (jnp.abs(above) + above) * 0.5
        if y == 0:
            by = jnp.where(tile == 0, 0.0, by)
        if y == ROWS - 1:
            ay = jnp.where(tile == TILES - 1, 0.0, ay)
        adj[2, y] = by
        adj[3, y] = ay
    def spread(i, before):
        for u in range(14):
            p = 14 * i + u
            c = pair_ref[0, p]
            values = (val[p] + valr[0, p]) + (valr[1, p] + valr[2, p])
            high, low = halves(ps[c] * (values * wgtr[c]))
            both = jnp.concatenate([high, low], axis=0)
            added = lax.dot_general(
                both, onehot[p], (((1,), (1,)), ((), ())), preferred_element_type=F32)
            before = before * pair_ref[3, p].astype(F32) + (added[:LV] + added[LV:])
            acc[p] = before
        return before

    total = jnp.zeros((LV, WIDE), F32)
    for part, (begin, end) in zip(copies, PARTS):
        wait_halo(part)
        total = lax.fori_loop(begin, end, spread, total)

    def place_gradient(y, j):
        w = 3 * y + j
        field[2, y + 1, :, WIDE * j:WIDE * j + WIDE] = acc[pair_ref[4, w]] * pair_ref[5, w].astype(F32)

    halo2 = []
    for j in range(3):
        for y in (0, ROWS - 1):
            place_gradient(y, j)
        halo2.append(halo_part(field.at[2], j, second_s, second_r))
    for y in INNER_FIRST[:6]:
        for j in range(3):
            place_gradient(y, j)
    def finish(y, v):
        rows = slice(LEVB * v, LEVB * v + LEVB)
        field[1, y + 1, rows, :] = stencil(3, y, v, 1) + field[0, y + 1, rows, :]

    def finish_inner():
        for y in INNER_FIRST[:6]:
            for v in range(VARS):
                finish(y, v)

    solve(1, 1, 2, halo2, into_field(3), finish_inner)
    outs = []
    for v in range(VARS):
        for y in INNER_FIRST[6:]:
            finish(y, v)
        out_stage = inc_ref.at[v]
        out_stage[...] = jnp.swapaxes(field[1, 1:ROWS + 1, LEVB * v:LEVB * v + LEVB, :], 0, 1)
        outs.append(pltpu.make_async_copy(out_stage, out_ref.at[:, v], out_sem.at[v]))
        outs[-1].start()
    for copy in outs:
        copy.wait()
    for copy in sent:
        copy.wait_send()


def shards(
    increment, courant_x, courant_y, level_inverse, coupling, profile, send_column, send_block, send_count, obs_weight,
):
    vmem = pl.BlockSpec(memory_space=pltpu.VMEM)
    any_space = pl.BlockSpec(memory_space=pl.ANY)
    smem = pl.BlockSpec(memory_space=pltpu.SMEM)
    dma = pltpu.SemaphoreType.DMA
    return pl.pallas_call(
        kernel,
        out_shape=jax.ShapeDtypeStruct(increment.shape, F32),
        in_specs=[any_space] * 3 + [vmem] * 5 + [smem] * 2,
        out_specs=any_space,
        scratch_shapes=[
            pltpu.VMEM((4, ROWS + 2, LV, NX), F32),
            pltpu.VMEM((ROWS + 2, LEVB, NX), F32),
            pltpu.VMEM((5, ROWS, LEVB, NX), F32),
            pltpu.VMEM((4, ROWS, LEVB, NX), F32),
            pltpu.VMEM((2, LV, NX), F32),
            pltpu.VMEM((2, ROWS, 12, 8, NX), F32),
            pltpu.VMEM((2, 3 * LV, NX), BF16),
            pltpu.VMEM((2, LV + 16, 3 * LV), BF16),
            pltpu.VMEM((2, 128, 128), F32),
            pltpu.VMEM((2, 2, LV, 128), F32),
            pltpu.VMEM((LV, 128), F32),
            pltpu.VMEM((12, 8, 128), F32),
            pltpu.VMEM((3, 8, 128), F32),
            pltpu.VMEM((2, 2, VARS * ROWS, NX), F32),
            pltpu.VMEM((2, 3, VARS * ROWS, NX), F32),
            pltpu.VMEM((2, 2, 11, 8, NX), F32),
            pltpu.VMEM((2, 2, 3, 8, NX), F32),
            pltpu.VMEM((4, 3, 8, 128), F32),
            pltpu.VMEM((64, 1, 128), F32),
            pltpu.VMEM((64, 128), F32),
            pltpu.VMEM((128, 128), F32),
            pltpu.VMEM((128, 128), jnp.int32),
            pltpu.VMEM((CHUNKS, 1, CHUNK), jnp.int32),
            pltpu.VMEM((CHUNKS, 1, CHUNK), F32),
            pltpu.VMEM((8, 128), jnp.int32),
            pltpu.VMEM((CHUNKS, LV, CHUNK), F32),
            pltpu.VMEM((WINDOWS, 2 * LV, WIDE), BF16),
            pltpu.VMEM((PAIRS, WIDE, CHUNK), BF16),
            pltpu.VMEM((PAIRS, 1, CHUNK), F32),
            pltpu.VMEM((3, PAIRS, 1, CHUNK), F32),
            pltpu.VMEM((PAIRS, LV, WIDE), F32),
            pltpu.VMEM((VARS, LEVB, ROWS, NX), F32),
            pltpu.VMEM((LEVB, ROWS, NX), F32),
            pltpu.VMEM((LEVB, ROWS, NX), F32),
            pltpu.SMEM((8, 128), jnp.int32),
            dma((2, 3)), dma((2, 3)), dma((2, 3)), dma((2, 3)), dma((2, 2, 3)), dma((2, 2, 3)), dma((2, 2, 3)), dma((2, 2, 3)),
            dma((2,)), dma((2,)), dma((3,)), dma((3,)),
            dma((2, 3, 2)), dma((2, 3, 2)), dma((4, 3)), dma((4, 3)), dma((TILES - 1,)), dma((TILES - 1,)),
            dma((3,)), dma((3,)),
            dma, dma((VARS,)), dma((VARS + 2,)),
        ],
        compiler_params=pltpu.CompilerParams(
            collective_id=0, has_side_effects=True, vmem_limit_bytes=56 * 1024 * 1024),
    )(
        increment, courant_x, courant_y, level_inverse, profile.transpose(1, 0, 2),
        send_column.reshape(64, 128), send_block.reshape(64, 128), obs_weight.reshape(64, 1, 128),
        coupling, send_count,
    )


def solution(mesh):
    return jax.shard_map(
        shards,
        mesh=mesh,
        in_specs=(
            P("band", None, "tile", None),
            P("band", "tile", None),
            P("band", "tile", None),
            P(None, "band", None),
            P(),
            P("band", None, None),
            P("tile", None),
            P("tile", None),
            P("tile", None),
            P("tile", None),
        ),
        out_specs=P("band", None, "tile", None),
        check_vma=False,
    )
```
